32 devices in a mesh: tracer: 4 (over y, x), domain: 8 (over z, core).
Axes of the slice: x: 2, y: 2, z: 4, core: 2. Of those that a mesh axis runs over, the one named last changes fastest.
Arguments:
- log_rate: float32 [128, 256, 256], P('domain'), may hold values from -1.6 to 0
- velocity: float32 [256, 256], replicated, may hold values from 0.2 to 1
- initial: float32 [4, 128, 256, 256], P('tracer', 'domain'), may hold values from -6 to 6
- profile: float32 [4, 256, 256], P('tracer'), may hold values from 0.5 to 4
- plane: int32 [4], P('tracer'), may hold values from 0 to 127
- depth: int32 [4, 32768], P('tracer'), may hold values from 0 to 127
- row: int32 [4, 32768], P('tracer'), may hold values from 0 to 255
- column: int32 [4, 32768], P('tracer'), may hold values from 0 to 255
- step_of: int32 [4, 32768], P('tracer'), may hold values from 1 to 2
- observed: float32 [4, 32768], P('tracer'), may hold values from -6 to 6
Outputs:
- smoothed_gradient: float32 [64, 128, 128], P('domain', 'tracer')
The draws below stay inside these ranges and needn't reach their ends.
All inputs are finite; a program needn't handle non-finite values.
Results may differ from the reference program's by a relative error of at most 0.0003.
Values sent between devices are 32-bit elements; how exact they have to be, the bound alone decides.
A program may use at most 512 MiB of HBM per device.

```python
import functools
import math
import jax
import jax.numpy as jnp
from jax import lax

R = 2
STEPS = 2
PROBES = 32768
FX = 256
FY = 256
FZ = 128
TRACERS = 4


def with_ends(values, stream_key, smallest, top_value):
    longest = values.shape.index(max(values.shape))
    spots = []
    for shift in (0, 1):
        where = [jax.random.randint(jax.random.fold_in(stream_key, axis), (), 0, length) for axis, length in enumerate(values.shape)]
        where[longest] = (where[longest] + shift) % values.shape[longest]
        spots.append(tuple(where))
    return values.at[spots[0]].set(smallest).at[spots[1]].set(top_value)


def block_levels(stream_key, shape, split, least, high):
    def one(axis_at, blocks):
        draws = jax.random.uniform(jax.random.fold_in(jax.random.fold_in(stream_key, 6), axis_at), (blocks,), jnp.float32, least / len(split), high / len(split))
        return jnp.repeat(jnp.exp(draws), shape[axis_at] // blocks).reshape((-1,) + (1,) * (len(shape) - axis_at - 1))

    factor_of = one(*split[0])
    for cut in split[1:]:
        factor_of = factor_of * one(*cut)
    return factor_of


def noise(own_key, dims, width, limit, split=(), kind=jnp.bfloat16):
    values = width * jax.random.normal(own_key, dims, jnp.float32)
    if split:
        values = values * block_levels(own_key, dims, split, -0.22, 0.18)
    return jnp.clip(values, -limit, limit).astype(kind)


def setup_inputs(seed: int = 0) -> dict:
    arg_keys = jax.random.split(jax.random.key(seed), 11)
    return {
        "log_rate": jnp.clip(-1.6 + 1.6 * jax.random.uniform(arg_keys[0], (FZ, FX, FY), jnp.float32) ** block_levels(arg_keys[0], (FZ, FX, FY), ((0, 8),), -0.2, 0.2), -1.6, 0.0),
        "velocity": jnp.clip(jax.random.uniform(arg_keys[1], (FX, FY), jnp.float32, 0.2, 1.0), 0.2, 1.0),
        "initial": noise(arg_keys[2], (TRACERS, FZ, FX, FY), 1.0, 6.0, ((0, 4), (1, 8)), jnp.float32),
        "profile": jnp.clip(jnp.exp(math.log(4.0) - 2.0794415 * jax.random.uniform(arg_keys[3], (TRACERS, FX, FY), jnp.float32) ** block_levels(arg_keys[3], (TRACERS, FX, FY), ((0, 4),), -0.2, 0.2)), 0.5, 4.0),
        "plane": with_ends(jax.random.randint(arg_keys[4], (TRACERS,), 0, FZ), jax.random.fold_in(arg_keys[4], 1), 0, FZ - 1).astype(jnp.int32),
        "depth": with_ends(jax.random.randint(arg_keys[5], (TRACERS, PROBES), 0, FZ), jax.random.fold_in(arg_keys[5], 1), 0, FZ - 1).astype(jnp.int32),
        "row": with_ends(jax.random.randint(arg_keys[6], (TRACERS, PROBES), 0, FX), jax.random.fold_in(arg_keys[6], 1), 0, FX - 1).astype(jnp.int32),
        "column": with_ends(jax.random.randint(arg_keys[7], (TRACERS, PROBES), 0, FY), jax.random.fold_in(arg_keys[7], 1), 0, FY - 1).astype(jnp.int32),
        "step_of": with_ends(jax.random.randint(arg_keys[8], (TRACERS, PROBES), 1, STEPS + 1), jax.random.fold_in(arg_keys[8], 1), 1, STEPS).astype(jnp.int32),
        "observed": noise(arg_keys[9], (TRACERS, PROBES), 1.0, 6.0, ((0, 4),), jnp.float32),
    }


TIME_STEP = 0.14
PRIOR_RANGE = 4.0


def face_rates(kappa_field):
    return [0.5 * (kappa_field + jnp.roll(kappa_field, -1, axis_dim)) for axis_dim in range(3)]


def diffusion(values, faces):
    result = jnp.zeros_like(values)
    for axis_dim in range(3):
        ahead_cell = jnp.roll(values, -1, axis_dim)
        behind_cell = jnp.roll(values, 1, axis_dim)
        result = result + faces[axis_dim] * (ahead_cell - values) - jnp.roll(faces[axis_dim], 1, axis_dim) * (values - behind_cell)
    return result


def sensitivity(state, adjoint):
    result = jnp.zeros_like(state)
    for axis_dim in range(3):
        product = (jnp.roll(state, -1, axis_dim) - state) * (jnp.roll(adjoint, -1, axis_dim) - adjoint)
        result = result + product + jnp.roll(product, 1, axis_dim)
    return -0.5 * result


def one_tracer(kappa_field, faces, velocity, items):
    initial, profile, plane, depth, row, column, step_of, observed = items
    depth_count, rows_count, cols_count = initial.shape
    layers = lax.iota(jnp.int32, depth_count)
    source = jnp.where((layers == plane)[:, None, None], profile[None], 0.0)
    wind = velocity[None]
    flat = depth * (rows_count * cols_count) + row * cols_count + column
    states = []
    values = initial
    sampled = jnp.zeros_like(observed)
    for section in range(STEPS):
        states.append(values)
        values = values + TIME_STEP * (diffusion(values, faces) - wind * (values - jnp.roll(values, 1, 0))) + TIME_STEP * source
        sampled = jnp.where(step_of == section + 1, values.reshape(-1)[flat], sampled)
    residual = sampled - observed

    def inject(section):
        empty = jnp.zeros((depth_count * rows_count * cols_count,), initial.dtype)
        return empty.at[flat].add(jnp.where(step_of == section, residual, 0.0)).reshape(initial.shape)

    adjoint = inject(STEPS)
    gradient = jnp.zeros_like(initial)
    for section in reversed(range(STEPS)):
        gradient = gradient + sensitivity(states[section], adjoint)
        if section > 0:
            adjoint = adjoint + TIME_STEP * (diffusion(adjoint, faces) - wind * (adjoint - jnp.roll(adjoint, -1, 0))) + inject(section)
    fine_grad = TIME_STEP * kappa_field * gradient
    return fine_grad.reshape(depth_count // R, R, rows_count // R, R, cols_count // R, R).sum(axis=(1, 3, 5))


def symbol_of(length):
    angles = (2.0 * math.pi / length) * lax.iota(jnp.float32, length)
    return 2.0 - 2.0 * jnp.cos(angles)


def prior_filter(shape):
    lam_sum = symbol_of(shape[0])[:, None, None] + symbol_of(shape[1])[None, :, None] + symbol_of(shape[2])[None, None, :]
    factor = 1.0 + PRIOR_RANGE * lam_sum
    return 1.0 / (factor * factor)


def reference(log_rate, velocity, initial, profile, plane, depth, row, column, step_of, observed):
    kappa_field = jnp.exp(log_rate)
    faces = face_rates(kappa_field)
    worker = functools.partial(one_tracer, kappa_field, faces, velocity)
    partials = lax.map(worker, (initial, profile, plane, depth, row, column, step_of, observed))
    summed = jnp.sum(partials, axis=0)
    spectrum = jnp.fft.fftn(summed)
    smoothed = jnp.real(jnp.fft.ifftn(spectrum * prior_filter(summed.shape)))
    return smoothed.astype(summed.dtype)
```

```python
import functools
import math

import jax
import jax.numpy as jnp
from jax import lax
from jax.experimental import pallas as pl
from jax.experimental.pallas import tpu as pltpu
from jax.sharding import PartitionSpec as P

R = 2
STEPS = 2
HALO = 2 * STEPS
STRIP = 64
LANES = 128

TIME_STEP = 0.14
PRIOR_RANGE = 4.0


def log2_of(size):
    bits = size.bit_length() - 1
    assert size == 1 << bits
    return bits


def sort_kernel(bits, key_in, value_in, keys, values):
    keys[...] = key_in[...]
    values[...] = value_in[...]
    blocks = keys.shape[0]
    group = min(8, blocks)

    def index_of(first, count):
        shape = (count, 8, LANES)
        return (
            (first + lax.broadcasted_iota(jnp.int32, shape, 0)) * (8 * LANES)
            + lax.broadcasted_iota(jnp.int32, shape, 1) * LANES
            + lax.broadcasted_iota(jnp.int32, shape, 2)
        )

    def far(distance, span):
        for first in range(0, blocks, 2 * distance):
            for start in range(first, first + distance, group):
                count = min(group, distance)
                low, high = pl.ds(start, count), pl.ds(start + distance, count)
                a, b, x, y = keys[low], keys[high], values[low], values[high]
                up = (index_of(start, count) & span) == 0
                swap = (up & (a > b)) | (jnp.logical_not(up) & (b > a))
                keys[low] = jnp.where(swap, b, a)
                keys[high] = jnp.where(swap, a, b)
                values[low] = jnp.where(swap, y, x)
                values[high] = jnp.where(swap, x, y)

    def near(axis, shift, bit, span):
        size = 8 if axis == 1 else LANES
        for start in range(0, blocks, group):
            part = pl.ds(start, group)
            a, x = keys[part], values[part]
            index = index_of(start, group)
            upper = (index & bit) != 0
            keep_min = ((index & span) == 0) != upper

            def partner(v):
                return jnp.where(
                    upper, pltpu.roll(v, shift, axis), pltpu.roll(v, size - shift, axis)
                )

            b, y = partner(a), partner(x)
            swap = (keep_min & (b < a)) | (jnp.logical_not(keep_min) & (b > a))
            keys[part] = jnp.where(swap, b, a)
            values[part] = jnp.where(swap, y, x)

    @pl.loop(0, bits)
    def _(phase):
        span = jnp.left_shift(jnp.int32(1), phase + 1)
        for q in reversed(range(bits)):

            @pl.when(q <= phase)
            def _():
                bit = 1 << q
                if bit >= 8 * LANES:
                    far(bit // (8 * LANES), span)
                elif bit >= LANES:
                    near(1, bit // LANES, bit, span)
                else:
                    near(2, bit, bit, span)


def sort_probes(keys, values):
    count = keys.shape[0]
    bits = log2_of(count)
    shape = (count // (8 * LANES), 8, LANES)
    spec = pl.BlockSpec(memory_space=pltpu.VMEM)
    keys, values = pl.pallas_call(
        functools.partial(sort_kernel, bits),
        out_shape=(
            jax.ShapeDtypeStruct(shape, jnp.int32),
            jax.ShapeDtypeStruct(shape, jnp.float32),
        ),
        in_specs=[spec, spec],
        out_specs=(spec, spec),
        cost_estimate=pl.CostEstimate(
            flops=count * 2000, bytes_accessed=count * 16, transcendentals=0
        ),
        name="sort_probes",
    )(keys.reshape(shape), values.reshape(shape))
    return keys.reshape(count // LANES, LANES), values.reshape(count // LANES, LANES)


def field_kernel(
    place,
    starts,
    keys,
    values,
    velocity,
    profile,
    rate_ref,
    rate_low,
    rate_high,
    init_ref,
    init_low,
    init_high,
    out,
    kappa,
    state0,
    state1,
    adjoint2,
    adjoint1,
    face_z,
    face_x,
    face_y,
    wind,
    counts,
    sums,
    sems,
):
    slab, rows, cols = rate_ref.shape
    planes = slab + 2 * HALO
    col_bits = log2_of(cols)
    row_bits = log2_of(rows)
    copies = []
    for number, (own, low, high, target) in enumerate(
        ((rate_ref, rate_low, rate_high, kappa), (init_ref, init_low, init_high, state0))
    ):
        for part, (source, first, count) in enumerate(
            ((own, HALO, slab), (low, 0, HALO), (high, HALO + slab, HALO))
        ):
            copy = pltpu.make_async_copy(
                source, target.at[pl.ds(first, count)], sems.at[3 * number + part]
            )
            copy.start()
            copies.append(copy)
    for copy in copies:
        copy.wait()

    starting = range(0, rows, STRIP)
    half = 0.5 * TIME_STEP

    def window(ref, z, r, after=True):
        pieces = [ref[z, pl.ds((r - 8) % rows, 8), :], ref[z, pl.ds(r, STRIP), :]]
        if after:
            pieces.append(ref[z, pl.ds((r + STRIP) % rows, 8), :])
        return jnp.concatenate(pieces, axis=0)

    def steps_down(wide):
        return (pltpu.roll(wide, wide.shape[0] - 1, 0) - wide)[: STRIP + 8]

    def with_previous(flux):
        return flux[8:], pltpu.roll(flux, 1, 0)[8:]

    def ahead(v):
        return pltpu.roll(v, cols - 1, 1)

    def behind(v):
        return pltpu.roll(v, 1, 1)

    @pl.loop(0, planes)
    def _(z):
        for r in starting:
            part = pl.ds(r, STRIP)
            kappa[z, part, :] = jnp.exp(kappa[z, part, :])

    @pl.loop(0, planes - 1)
    def _(z):
        for r in starting:
            part = pl.ds(r, STRIP)
            wide = window(kappa, z, r)
            k = wide[8 : 8 + STRIP]
            face_z[z, part, :] = half * (k + kappa[z + 1, part, :])
            face_x[z, part, :] = half * (k + pltpu.roll(wide, STRIP + 15, 0)[8 : 8 + STRIP])
            face_y[z, part, :] = half * (k + ahead(k))

    for r in starting:
        part = pl.ds(r, STRIP)
        wind[part, :] = TIME_STEP * velocity[part, :]

    def stepped(ref, z, r, forward):
        part = pl.ds(r, STRIP)
        wide = window(ref, z, r)
        v = wide[8 : 8 + STRIP]
        upper, lower = face_z[z, part, :], face_z[z - 1, part, :]
        if forward:
            lower = lower + wind[part, :]
        else:
            upper = upper + wind[part, :]
        total = upper * (ref[z + 1, part, :] - v) - lower * (v - ref[z - 1, part, :])
        flux, previous = with_previous(window(face_x, z, r, False) * steps_down(wide))
        total = total + (flux - previous)
        flux = face_y[z, part, :] * (ahead(v) - v)
        return v + (total + (flux - behind(flux)))

    source_plane = place[0]

    def forward(ref, z, r):
        scale = jnp.where(z == source_plane, jnp.float32(TIME_STEP), jnp.float32(0.0))
        return stepped(ref, z, r, True) + scale * profile[pl.ds(r, STRIP), :]

    @pl.loop(1, planes - 1)
    def _(z):
        for r in starting:
            state1[z, pl.ds(r, STRIP), :] = forward(state0, z, r)

    blocks = keys.shape[0]
    span = 2 * LANES
    lane_rows = lax.broadcasted_iota(jnp.int32, (rows, span), 0)
    lane_cols = lax.broadcasted_iota(jnp.int32, (cols, span), 0)

    def gather_plane(bucket):
        first, last = starts[bucket], starts[bucket + 1]
        block = first // LANES

        def partial(number):
            at = [jnp.minimum(number + i, blocks - 1) for i in range(2)]
            own = [
                jnp.right_shift(keys[pl.ds(at[i], 1), :], col_bits + row_bits)
                == jnp.where(number + i < blocks, bucket, -1)
                for i in range(2)
            ]
            key = [keys[pl.ds(i, 1), :] for i in at]
            row = jnp.concatenate(
                [
                    jnp.where(mine, jnp.right_shift(k, col_bits) & (rows - 1), -1)
                    for mine, k in zip(own, key)
                ],
                axis=1,
            )
            col = jnp.concatenate(key, axis=1) & (cols - 1)
            value = jnp.concatenate([values[pl.ds(i, 1), :] for i in at], axis=1)
            high = value.astype(jnp.bfloat16).astype(jnp.float32)
            rest = value - high
            row_hot = jnp.where(lane_rows == row, 1.0, 0.0).astype(jnp.bfloat16)
            col_hit = lane_cols == col

            def hot(v):
                return jnp.where(col_hit, v, 0.0).astype(jnp.bfloat16)

            def product(a, b):
                return lax.dot_general(
                    a, b, (((1,), (1,)), ((), ())), preferred_element_type=jnp.float32
                )

            return product(row_hot, hot(1.0)), product(
                jnp.concatenate([row_hot, row_hot], axis=1),
                jnp.concatenate([hot(high), hot(rest)], axis=1),
            )

        counts[...], sums[...] = partial(block)

        @pl.loop(1, jnp.maximum((last + span - 1 - block * LANES) // span, 1))
        def _(number):
            count, total = partial(block + 2 * number)
            counts[...] += count
            sums[...] += total

    @pl.loop(2, planes - 2)
    def _(z):
        gather_plane(planes + z)
        for r in starting:
            part = pl.ds(r, STRIP)
            adjoint2[z, part, :] = counts[part, :] * forward(state1, z, r) - sums[part, :]

    @pl.loop(3, planes - 3)
    def _(z):
        gather_plane(z)
        for r in starting:
            part = pl.ds(r, STRIP)
            inject = counts[part, :] * state1[z, part, :] - sums[part, :]
            adjoint1[z, part, :] = stepped(adjoint2, z, r, False) + inject

    fields = ((state1, adjoint2), (state0, adjoint1))

    def upward(z, part):
        return sum(
            (state[z + 1, part, :] - state[z, part, :])
            * (adjoint[z + 1, part, :] - adjoint[z, part, :])
            for state, adjoint in fields
        )

    def level(z, r):
        wide = [(window(state, z, r), window(adjoint, z, r)) for state, adjoint in fields]
        flux, previous = with_previous(sum(steps_down(c) * steps_down(m) for c, m in wide))
        total = flux + previous
        inner = [(c[8 : 8 + STRIP], m[8 : 8 + STRIP]) for c, m in wide]
        flux = sum((ahead(c) - c) * (ahead(m) - m) for c, m in inner)
        return total + (flux + behind(flux))

    def pool(length):
        shape = (length, length // R)
        fine = lax.broadcasted_iota(jnp.int32, shape, 0)
        coarse = lax.broadcasted_iota(jnp.int32, shape, 1)
        return jnp.where((fine >= coarse * R) & (fine < coarse * R + R), 1.0, 0.0)

    def exact(a, b, dims):
        return lax.dot_general(
            a,
            b,
            (dims, ((), ())),
            precision=lax.Precision.HIGHEST,
            preferred_element_type=jnp.float32,
        )

    @pl.loop(0, slab // R)
    def _(number):
        for r in starting:
            part = pl.ds(r, STRIP)
            both = jnp.zeros((STRIP, cols), jnp.float32)
            below = upward(HALO + number * R - 1, part)
            for layer in range(R):
                z = HALO + number * R + layer
                above = upward(z, part)
                both = both + kappa[z, part, :] * (level(z, r) + (below + above))
                below = above
            sums[part, :] = (-half) * both
        narrow = exact(sums[...], pool(cols), ((1,), (0,)))
        out[number] = exact(pool(rows), narrow, ((0,), (0,)))


def fields(place, starts, keys, values, velocity, profile, rates, inits):
    slab, rows, cols = rates[0].shape
    planes = slab + 2 * HALO
    smem = pl.BlockSpec(memory_space=pltpu.SMEM)
    vmem = pl.BlockSpec(memory_space=pltpu.VMEM)
    hbm = pl.BlockSpec(memory_space=pl.ANY)
    field = pltpu.VMEM((planes, rows, cols), jnp.float32)
    plane = pltpu.VMEM((rows, cols), jnp.float32)
    return pl.pallas_call(
        field_kernel,
        out_shape=jax.ShapeDtypeStruct((slab // R, rows // R, cols // R), jnp.float32),
        in_specs=[smem, smem] + [vmem] * 4 + [hbm] * 6,
        out_specs=vmem,
        scratch_shapes=[field] * 8 + [plane] * 3 + [pltpu.SemaphoreType.DMA((6,))],
        compiler_params=pltpu.CompilerParams(vmem_limit_bytes=60 * 1024 * 1024),
        cost_estimate=pl.CostEstimate(
            flops=planes * rows * cols * 200,
            bytes_accessed=planes * rows * cols * 8,
            transcendentals=planes * rows * cols,
        ),
        name="fields",
    )(place, starts, keys, values, velocity, profile, *rates, *inits)


def halos(array, axis, width):
    count, length = lax.axis_size(axis), array.shape[0]
    up = [(i, (i + 1) % count) for i in range(count)]
    down = [(j, i) for i, j in up]
    before = lax.ppermute(array[length - width :], axis, up)
    after = lax.ppermute(array[:width], axis, down)
    return array, before, after


def hartley(length, first_row, count):
    indices = first_row + lax.iota(jnp.int32, count)
    phases = indices[:, None] * lax.iota(jnp.int32, length)[None, :] % length
    angles = 2.0 * math.pi / length * phases.astype(jnp.float32)
    return jnp.cos(angles) + jnp.sin(angles)


def transform(table, values, axis_dim):
    forms = ("kj,jab->kab", "kj,ajb->akb", "kj,abj->abk")
    return jnp.einsum(
        forms[axis_dim],
        table,
        values,
        precision=lax.Precision.HIGHEST,
        preferred_element_type=jnp.float32,
    )


def symbol_part(length, first_row, count):
    indices = (first_row + lax.iota(jnp.int32, count)) % length
    angles = 2.0 * math.pi / length * indices.astype(jnp.float32)
    return 2.0 - 2.0 * jnp.cos(angles)


def local(log_rate, velocity, initial, profile, plane, depth, row, column, step_of, observed):
    slab, rows, cols = log_rate.shape
    domains, tracers = lax.axis_size("domain"), lax.axis_size("tracer")
    full = slab * domains
    planes = slab + 2 * HALO
    first = lax.axis_index("domain") * slab - HALO
    rates = halos(log_rate, "domain", HALO)
    inits = halos(initial[0], "domain", HALO)

    layer = (depth[0] - first + full) % full
    bucket = jnp.where(layer < planes, (step_of[0] - 1) * planes + layer, STEPS * planes)
    keys = bucket * (rows * cols) + row[0] * cols + column[0]
    edges = lax.iota(jnp.int32, STEPS * planes + 1)
    starts = jnp.sum((bucket[None, :] < edges[:, None]).astype(jnp.int32), axis=1)
    keys, values = sort_probes(keys, observed[0])
    place = (plane - first + full) % full

    coarse = fields(place, starts, keys, values, velocity, profile[0], rates, inits)

    x_size, y_size = coarse.shape[1:]
    z_size = full // R
    x_table = hartley(x_size, 0, x_size)
    y_table = hartley(y_size, 0, y_size)
    z_table = hartley(z_size, 0, z_size)
    x_share, y_share, x_block = x_size // tracers, y_size // tracers, x_size // domains

    spectral = transform(y_table, coarse, 2)
    spectral = jnp.swapaxes(spectral, 1, 2)
    parts = spectral.reshape(slab // R, tracers, y_share, x_size)
    parts = lax.all_to_all(parts, "tracer", split_axis=1, concat_axis=1, tiled=True)
    spectral = transform(x_table, parts.sum(axis=1), 2)
    spectral = spectral.reshape(slab // R, y_share, domains, x_block)
    spectral = jnp.moveaxis(spectral, 2, 0)
    spectral = lax.all_to_all(spectral, "domain", split_axis=0, concat_axis=0, tiled=True)
    columns = spectral.reshape(z_size, y_share * x_block)
    columns = jnp.dot(z_table, columns, precision=lax.Precision.HIGHEST)
    lam_z = symbol_part(z_size, 0, z_size)
    lam_y = symbol_part(y_size, lax.axis_index("tracer") * y_share, y_share)
    lam_x = symbol_part(x_size, lax.axis_index("domain") * x_block, x_block)
    lam = lam_z[:, None] + (lam_y[:, None] + lam_x[None, :]).reshape(1, -1)
    factor = 1.0 + PRIOR_RANGE * lam
    columns = columns * (1.0 / (factor * factor) / (x_size * y_size * z_size))
    columns = jnp.dot(z_table, columns, precision=lax.Precision.HIGHEST)
    columns = columns.reshape(domains, slab // R, y_share, x_block)
    columns = lax.all_to_all(columns, "domain", split_axis=0, concat_axis=0, tiled=True)
    columns = jnp.moveaxis(columns, 0, 2).reshape(slab // R, y_share, x_size)
    columns = transform(x_table, columns, 2)
    columns = columns.reshape(slab // R, y_share, tracers, x_share)
    columns = jnp.moveaxis(columns, 2, 0)
    columns = lax.all_to_all(columns, "tracer", split_axis=0, concat_axis=0, tiled=True)
    columns = jnp.moveaxis(columns, 0, 1).reshape(slab // R, y_size, x_share)
    return jnp.einsum(
        "kj,zjx->zxk",
        y_table,
        columns,
        precision=lax.Precision.HIGHEST,
        preferred_element_type=jnp.float32,
    )


def solution(mesh):
    return jax.shard_map(
        local,
        mesh=mesh,
        in_specs=(
            P("domain", None, None),
            P(),
            P("tracer", "domain", None, None),
            P("tracer", None, None),
            P("tracer"),
            P("tracer", None),
            P("tracer", None),
            P("tracer", None),
            P("tracer", None),
            P("tracer", None),
        ),
        out_specs=P("domain", "tracer", None),
        check_vma=False,
    )
```

```python
import functools
import math

import jax
import jax.numpy as jnp
from jax import lax
from jax.experimental import pallas as pl
from jax.experimental.pallas import tpu as pltpu
from jax.sharding import PartitionSpec as P

R = 2
STEPS = 2
HALO = 2 * STEPS
STRIP = 64
LANES = 128

TIME_STEP = 0.14
PRIOR_RANGE = 4.0


def log2_of(size):
    bits = size.bit_length() - 1
    assert size == 1 << bits
    return bits


def sort_kernel(bits, key_in, value_in, keys, values):
    keys[...] = key_in[...]
    values[...] = value_in[...]
    blocks = keys.shape[0]
    group = min(8, blocks)

    def index_of(first, count):
        shape = (count, 8, LANES)
        return (
            (first + lax.broadcasted_iota(jnp.int32, shape, 0)) * (8 * LANES)
            + lax.broadcasted_iota(jnp.int32, shape, 1) * LANES
            + lax.broadcasted_iota(jnp.int32, shape, 2)
        )

    def far(distance, span):
        for first in range(0, blocks, 2 * distance):
            for start in range(first, first + distance, group):
                count = min(group, distance)
                low, high = pl.ds(start, count), pl.ds(start + distance, count)
                a, b, x, y = keys[low], keys[high], values[low], values[high]
                up = (index_of(start, count) & span) == 0
                swap = (up & (a > b)) | (jnp.logical_not(up) & (b > a))
                keys[low] = jnp.where(swap, b, a)
                keys[high] = jnp.where(swap, a, b)
                values[low] = jnp.where(swap, y, x)
                values[high] = jnp.where(swap, x, y)

    def near(axis, shift, bit, span):
        size = 8 if axis == 1 else LANES
        for start in range(0, blocks, group):
            part = pl.ds(start, group)
            a, x = keys[part], values[part]
            index = index_of(start, group)
            upper = (index & bit) != 0
            keep_min = ((index & span) == 0) != upper

            def partner(v):
                return jnp.where(
                    upper, pltpu.roll(v, shift, axis), pltpu.roll(v, size - shift, axis)
                )

            b, y = partner(a), partner(x)
            swap = (keep_min & (b < a)) | (jnp.logical_not(keep_min) & (b > a))
            keys[part] = jnp.where(swap, b, a)
            values[part] = jnp.where(swap, y, x)

    @pl.loop(0, bits)
    def _(phase):
        span = jnp.left_shift(jnp.int32(1), phase + 1)
        for q in reversed(range(bits)):

            @pl.when(q <= phase)
            def _():
                bit = 1 << q
                if bit >= 8 * LANES:
                    far(bit // (8 * LANES), span)
                elif bit >= LANES:
                    near(1, bit // LANES, bit, span)
                else:
                    near(2, bit, bit, span)


def sort_probes(keys, values):
    count = keys.shape[0]
    bits = log2_of(count)
    shape = (count // (8 * LANES), 8, LANES)
    spec = pl.BlockSpec(memory_space=pltpu.VMEM)
    keys, values = pl.pallas_call(
        functools.partial(sort_kernel, bits),
        out_shape=(
            jax.ShapeDtypeStruct(shape, jnp.int32),
            jax.ShapeDtypeStruct(shape, jnp.float32),
        ),
        in_specs=[spec, spec],
        out_specs=(spec, spec),
        cost_estimate=pl.CostEstimate(
            flops=count * 2000, bytes_accessed=count * 16, transcendentals=0
        ),
        name="sort_probes",
    )(keys.reshape(shape), values.reshape(shape))
    return keys.reshape(count // LANES, LANES), values.reshape(count // LANES, LANES)


def field_kernel(
    place,
    starts,
    keys,
    values,
    velocity,
    profile,
    rate_ref,
    rate_low,
    rate_high,
    init_ref,
    init_low,
    init_high,
    out,
    kappa,
    state0,
    state1,
    adjoint2,
    adjoint1,
    face_z,
    face_x,
    face_y,
    wind,
    counts,
    sums,
    sems,
):
    slab, rows, cols = rate_ref.shape
    planes = slab + 2 * HALO
    col_bits = log2_of(cols)
    row_bits = log2_of(rows)
    copies = []
    for number, (own, low, high, target) in enumerate(
        ((rate_ref, rate_low, rate_high, kappa), (init_ref, init_low, init_high, state0))
    ):
        for part, (source, first, count) in enumerate(
            ((own, HALO, slab), (low, 0, HALO), (high, HALO + slab, HALO))
        ):
            copy = pltpu.make_async_copy(
                source, target.at[pl.ds(first, count)], sems.at[3 * number + part]
            )
            copy.start()
            copies.append(copy)
    for copy in copies:
        copy.wait()

    starting = range(0, rows, STRIP)
    half = 0.5 * TIME_STEP

    def window(ref, z, r, after=True):
        pieces = [ref[z, pl.ds((r - 8) % rows, 8), :], ref[z, pl.ds(r, STRIP), :]]
        if after:
            pieces.append(ref[z, pl.ds((r + STRIP) % rows, 8), :])
        return jnp.concatenate(pieces, axis=0)

    def steps_down(wide):
        return (pltpu.roll(wide, wide.shape[0] - 1, 0) - wide)[: STRIP + 8]

    def with_previous(flux):
        return flux[8:], pltpu.roll(flux, 1, 0)[8:]

    def ahead(v):
        return pltpu.roll(v, cols - 1, 1)

    def behind(v):
        return pltpu.roll(v, 1, 1)

    @pl.loop(0, planes)
    def _(z):
        for r in starting:
            part = pl.ds(r, STRIP)
            kappa[z, part, :] = jnp.exp(kappa[z, part, :])

    @pl.loop(0, planes - 1)
    def _(z):
        for r in starting:
            part = pl.ds(r, STRIP)
            wide = window(kappa, z, r)
            k = wide[8 : 8 + STRIP]
            face_z[z, part, :] = half * (k + kappa[z + 1, part, :])
            face_x[z, part, :] = half * (k + pltpu.roll(wide, STRIP + 15, 0)[8 : 8 + STRIP])
            face_y[z, part, :] = half * (k + ahead(k))

    for r in starting:
        part = pl.ds(r, STRIP)
        wind[part, :] = TIME_STEP * velocity[part, :]

    def stepped(ref, z, r, forward):
        part = pl.ds(r, STRIP)
        wide = window(ref, z, r)
        v = wide[8 : 8 + STRIP]
        upper, lower = face_z[z, part, :], face_z[z - 1, part, :]
        if forward:
            lower = lower + wind[part, :]
        else:
            upper = upper + wind[part, :]
        total = upper * (ref[z + 1, part, :] - v) - lower * (v - ref[z - 1, part, :])
        flux, previous = with_previous(window(face_x, z, r, False) * steps_down(wide))
        total = total + (flux - previous)
        flux = face_y[z, part, :] * (ahead(v) - v)
        return v + (total + (flux - behind(flux)))

    source_plane = place[0]

    def forward(ref, z, r):
        scale = jnp.where(z == source_plane, jnp.float32(TIME_STEP), jnp.float32(0.0))
        return stepped(ref, z, r, True) + scale * profile[pl.ds(r, STRIP), :]

    @pl.loop(1, planes - 1)
    def _(z):
        for r in starting:
            state1[z, pl.ds(r, STRIP), :] = forward(state0, z, r)

    blocks = keys.shape[0]
    span = 2 * LANES
    lane_rows = lax.broadcasted_iota(jnp.int32, (rows, span), 0)
    lane_cols = lax.broadcasted_iota(jnp.int32, (cols, span), 0)

    def gather_plane(bucket):
        first, last = starts[bucket], starts[bucket + 1]
        block = first // LANES

        def partial(number):
            at = [jnp.minimum(number + i, blocks - 1) for i in range(2)]
            own = [
                jnp.right_shift(keys[pl.ds(at[i], 1), :], col_bits + row_bits)
                == jnp.where(number + i < blocks, bucket, -1)
                for i in range(2)
            ]
            key = [keys[pl.ds(i, 1), :] for i in at]
            row = jnp.concatenate(
                [
                    jnp.where(mine, jnp.right_shift(k, col_bits) & (rows - 1), -1)
                    for mine, k in zip(own, key)
                ],
                axis=1,
            )
            col = jnp.concatenate(key, axis=1) & (cols - 1)
            value = jnp.concatenate([values[pl.ds(i, 1), :] for i in at], axis=1)
            high = value.astype(jnp.bfloat16).astype(jnp.float32)
            rest = value - high
            row_hot = jnp.where(lane_rows == row, 1.0, 0.0).astype(jnp.bfloat16)
            col_hit = lane_cols == col

            def hot(v):
                return jnp.where(col_hit, v, 0.0).astype(jnp.bfloat16)

            def product(a, b):
                return lax.dot_general(
                    a, b, (((1,), (1,)), ((), ())), preferred_element_type=jnp.float32
                )

            return product(row_hot, hot(1.0)), product(
                jnp.concatenate([row_hot, row_hot], axis=1),
                jnp.concatenate([hot(high), hot(rest)], axis=1),
            )

        counts[...], sums[...] = partial(block)

        @pl.loop(1, jnp.maximum((last + span - 1 - block * LANES) // span, 1))
        def _(number):
            count, total = partial(block + 2 * number)
            counts[...] += count
            sums[...] += total

    @pl.loop(2, planes - 2)
    def _(z):
        gather_plane(planes + z)
        for r in starting:
            part = pl.ds(r, STRIP)
            adjoint2[z, part, :] = counts[part, :] * forward(state1, z, r) - sums[part, :]

    @pl.loop(3, planes - 3)
    def _(z):
        gather_plane(z)
        for r in starting:
            part = pl.ds(r, STRIP)
            inject = counts[part, :] * state1[z, part, :] - sums[part, :]
            adjoint1[z, part, :] = stepped(adjoint2, z, r, False) + inject

    fields = ((state1, adjoint2), (state0, adjoint1))

    def upward(z, part):
        return sum(
            (state[z + 1, part, :] - state[z, part, :])
            * (adjoint[z + 1, part, :] - adjoint[z, part, :])
            for state, adjoint in fields
        )

    def level(z, r):
        wide = [(window(state, z, r), window(adjoint, z, r)) for state, adjoint in fields]
        flux, previous = with_previous(sum(steps_down(c) * steps_down(m) for c, m in wide))
        total = flux + previous
        inner = [(c[8 : 8 + STRIP], m[8 : 8 + STRIP]) for c, m in wide]
        flux = sum((ahead(c) - c) * (ahead(m) - m) for c, m in inner)
        return total + (flux + behind(flux))

    def pool(length):
        shape = (length, length // R)
        fine = lax.broadcasted_iota(jnp.int32, shape, 0)
        coarse = lax.broadcasted_iota(jnp.int32, shape, 1)
        return jnp.where((fine >= coarse * R) & (fine < coarse * R + R), 1.0, 0.0)

    def exact(a, b, dims):
        return lax.dot_general(
            a,
            b,
            (dims, ((), ())),
            precision=lax.Precision.HIGHEST,
            preferred_element_type=jnp.float32,
        )

    @pl.loop(0, slab // R)
    def _(number):
        for r in starting:
            part = pl.ds(r, STRIP)
            both = jnp.zeros((STRIP, cols), jnp.float32)
            below = upward(HALO + number * R - 1, part)
            for layer in range(R):
                z = HALO + number * R + layer
                above = upward(z, part)
                both = both + kappa[z, part, :] * (level(z, r) + (below + above))
                below = above
            sums[part, :] = (-half) * both
        narrow = exact(sums[...], pool(cols), ((1,), (0,)))
        out[number] = exact(pool(rows), narrow, ((0,), (0,)))


def fields(place, starts, keys, values, velocity, profile, rates, inits):
    slab, rows, cols = rates[0].shape
    planes = slab + 2 * HALO
    smem = pl.BlockSpec(memory_space=pltpu.SMEM)
    vmem = pl.BlockSpec(memory_space=pltpu.VMEM)
    hbm = pl.BlockSpec(memory_space=pl.ANY)
    field = pltpu.VMEM((planes, rows, cols), jnp.float32)
    plane = pltpu.VMEM((rows, cols), jnp.float32)
    return pl.pallas_call(
        field_kernel,
        out_shape=jax.ShapeDtypeStruct((slab // R, rows // R, cols // R), jnp.float32),
        in_specs=[smem, smem] + [vmem] * 4 + [hbm] * 6,
        out_specs=vmem,
        scratch_shapes=[field] * 8 + [plane] * 3 + [pltpu.SemaphoreType.DMA((6,))],
        compiler_params=pltpu.CompilerParams(vmem_limit_bytes=60 * 1024 * 1024),
        cost_estimate=pl.CostEstimate(
            flops=planes * rows * cols * 200,
            bytes_accessed=planes * rows * cols * 8,
            transcendentals=planes * rows * cols,
        ),
        name="fields",
    )(place, starts, keys, values, velocity, profile, *rates, *inits)


def tail_kernel(
    domains,
    tracers,
    coarse,
    weights,
    x_table,
    y_table,
    z_table,
    out,
    send_sum,
    recv_sum,
    send_z,
    recv_z,
    send_back,
    recv_back,
    send_x,
    recv_x,
    sum_sems,
    z_sems,
    back_sems,
    x_sems,
):
    depth, x_size, y_size = coarse.shape
    y_share, x_share = y_size // tracers, x_size // tracers
    y_own = y_share // domains
    z_size = depth * domains
    tracer, domain = lax.axis_index("tracer"), lax.axis_index("domain")

    barrier = pltpu.get_barrier_semaphore()
    for axis, me, count in (("tracer", tracer, tracers), ("domain", domain, domains)):
        for i in range(1, count):
            pl.semaphore_signal(
                barrier,
                inc=1,
                device_id={axis: lax.rem(me + i, count)},
                device_id_type=pl.DeviceIdType.MESH,
            )
    pl.semaphore_wait(barrier, tracers + domains - 2)

    def exact(a, b, dims):
        return lax.dot_general(
            a,
            b,
            (dims, ((), ())),
            precision=lax.Precision.HIGHEST,
            preferred_element_type=jnp.float32,
        )

    def exchange(axis, me, count, source, target, sems):
        copies = []
        for i in range(1, count):
            peer = lax.rem(me + i, count)
            copy = pltpu.make_async_remote_copy(
                src_ref=source(peer),
                dst_ref=target(i, me),
                send_sem=sems.at[0, i],
                recv_sem=sems.at[1, i],
                device_id={axis: peer},
                device_id_type=pl.DeviceIdType.MESH,
            )
            copy.start()
            copies.append(copy)
        return copies

    spectral = exact(y_table[...], coarse[...].reshape(depth * x_size, y_size), ((1,), (1,)))
    for block in range(tracers):
        send_sum[block] = spectral[block * y_share : (block + 1) * y_share]
    first = exchange(
        "tracer",
        tracer,
        tracers,
        lambda peer: send_sum.at[peer],
        lambda i, me: recv_sum.at[i],
        sum_sems,
    )
    total = send_sum[tracer]
    for i, copy in enumerate(first):
        copy.wait_recv()
        total = total + recv_sum[i + 1]

    for z in range(depth):
        send_z[:, z, :] = exact(
            total[:, z * x_size : (z + 1) * x_size], x_table[...], ((1,), (0,))
        )
    second = exchange(
        "domain",
        domain,
        domains,
        lambda peer: send_z.at[pl.ds(peer * y_own, y_own)],
        lambda i, me: recv_z.at[me],
        z_sems,
    )
    recv_z[domain] = send_z[pl.ds(domain * y_own, y_own)]
    for copy in second:
        copy.wait_recv()

    for k in range(y_own):
        column = recv_z[:, k].reshape(z_size, x_size)
        column = exact(z_table[...], column, ((1,), (0,))) * weights[k]
        column = exact(z_table[...], column, ((1,), (0,)))
        send_back[:, k] = column.reshape(domains, depth, x_size)
    third = exchange(
        "domain",
        domain,
        domains,
        lambda peer: send_back.at[peer],
        lambda i, me: recv_back.at[pl.ds(me * y_own, y_own)],
        back_sems,
    )
    recv_back[pl.ds(domain * y_own, y_own)] = send_back[domain]
    for copy in third:
        copy.wait_recv()

    spectral = jnp.concatenate([recv_back[:, z, :] for z in range(depth)], axis=0)
    spectral = exact(x_table[...], spectral, ((1,), (1,)))
    for block in range(tracers):
        send_x[block] = spectral[block * x_share : (block + 1) * x_share]
    fourth = exchange(
        "tracer",
        tracer,
        tracers,
        lambda peer: send_x.at[peer],
        lambda i, me: recv_x.at[me],
        x_sems,
    )
    recv_x[tracer] = send_x[tracer]
    for copy in fourth:
        copy.wait_recv()

    for z in range(depth):
        lanes = slice(z * y_share, (z + 1) * y_share)
        row = jnp.concatenate([recv_x[i][:, lanes] for i in range(tracers)], axis=1)
        out[z] = exact(row, y_table[...], ((1,), (0,)))
    for copy in first + second + third + fourth:
        copy.wait_send()


def filtered(coarse, weights, x_table, y_table, z_table):
    depth, x_size, y_size = coarse.shape
    domains, tracers = lax.axis_size("domain"), lax.axis_size("tracer")
    y_share, x_share = y_size // tracers, x_size // tracers
    y_own = y_share // domains
    vmem = pl.BlockSpec(memory_space=pltpu.VMEM)

    def buffer(*shape):
        return pltpu.VMEM(shape, jnp.float32)

    def sems(count):
        return pltpu.SemaphoreType.DMA((2, count))

    return pl.pallas_call(
        functools.partial(tail_kernel, domains, tracers),
        out_shape=jax.ShapeDtypeStruct((depth, x_share, y_size), jnp.float32),
        in_specs=[vmem] * 5,
        out_specs=vmem,
        scratch_shapes=[
            buffer(tracers, y_share, depth * x_size),
            buffer(tracers, y_share, depth * x_size),
            buffer(y_share, depth, x_size),
            buffer(domains, y_own, depth, x_size),
            buffer(domains, y_own, depth, x_size),
            buffer(y_share, depth, x_size),
            buffer(tracers, x_share, depth * y_share),
            buffer(tracers, x_share, depth * y_share),
            sems(tracers),
            sems(domains),
            sems(domains),
            sems(tracers),
        ],
        compiler_params=pltpu.CompilerParams(
            collective_id=1, has_side_effects=True, vmem_limit_bytes=24 * 1024 * 1024
        ),
        cost_estimate=pl.CostEstimate(
            flops=coarse.size * 3000, bytes_accessed=coarse.size * 8, transcendentals=0
        ),
        name="filtered",
    )(coarse, weights, x_table, y_table, z_table)


def halos(array, axis, width):
    count, length = lax.axis_size(axis), array.shape[0]
    up = [(i, (i + 1) % count) for i in range(count)]
    down = [(j, i) for i, j in up]
    before = lax.ppermute(array[length - width :], axis, up)
    after = lax.ppermute(array[:width], axis, down)
    return array, before, after


def hartley(length, first_row, count):
    indices = first_row + lax.iota(jnp.int32, count)
    phases = indices[:, None] * lax.iota(jnp.int32, length)[None, :] % length
    angles = 2.0 * math.pi / length * phases.astype(jnp.float32)
    return jnp.cos(angles) + jnp.sin(angles)


def symbol_part(length, first_row, count):
    indices = (first_row + lax.iota(jnp.int32, count)) % length
    angles = 2.0 * math.pi / length * indices.astype(jnp.float32)
    return 2.0 - 2.0 * jnp.cos(angles)


def local(log_rate, velocity, initial, profile, plane, depth, row, column, step_of, observed):
    slab, rows, cols = log_rate.shape
    domains, tracers = lax.axis_size("domain"), lax.axis_size("tracer")
    full = slab * domains
    planes = slab + 2 * HALO
    first = lax.axis_index("domain") * slab - HALO
    rates = halos(log_rate, "domain", HALO)
    inits = halos(initial[0], "domain", HALO)

    layer = (depth[0] - first + full) % full
    bucket = jnp.where(layer < planes, (step_of[0] - 1) * planes + layer, STEPS * planes)
    keys = bucket * (rows * cols) + row[0] * cols + column[0]
    edges = lax.iota(jnp.int32, STEPS * planes + 1)
    starts = jnp.sum((bucket[None, :] < edges[:, None]).astype(jnp.int32), axis=1)
    keys, values = sort_probes(keys, observed[0])
    place = (plane - first + full) % full

    coarse = fields(place, starts, keys, values, velocity, profile[0], rates, inits)

    x_size, y_size, z_size = rows // R, cols // R, full // R
    y_own = y_size // (tracers * domains)
    own_first = (lax.axis_index("tracer") * domains + lax.axis_index("domain")) * y_own
    lam = (
        symbol_part(y_size, own_first, y_own)[:, None, None]
        + symbol_part(z_size, 0, z_size)[None, :, None]
        + symbol_part(x_size, 0, x_size)[None, None, :]
    )
    factor = 1.0 + PRIOR_RANGE * lam
    weights = 1.0 / (factor * factor) / (x_size * y_size * z_size)
    tables = [hartley(size, 0, size) for size in (x_size, y_size, z_size)]
    return filtered(coarse, weights, *tables)


def solution(mesh):
    return jax.shard_map(
        local,
        mesh=mesh,
        in_specs=(
            P("domain", None, None),
            P(),
            P("tracer", "domain", None, None),
            P("tracer", None, None),
            P("tracer"),
            P("tracer", None),
            P("tracer", None),
            P("tracer", None),
            P("tracer", None),
            P("tracer", None),
        ),
        out_specs=P("domain", "tracer", None),
        check_vma=False,
    )
```

```python
import functools
import math

import jax
import jax.numpy as jnp
from jax import lax
from jax.experimental import pallas as pl
from jax.experimental.pallas import tpu as pltpu
from jax.sharding import PartitionSpec as P

R = 2
STEPS = 2
HALO = 2 * STEPS
STRIP = 64
LANES = 128
AHEAD = 4

TIME_STEP = 0.14
PRIOR_RANGE = 4.0


def log2_of(size):
    bits = size.bit_length() - 1
    assert size == 1 << bits
    return bits


def sort_kernel(bits, key_in, value_in, keys, values):
    keys[...] = key_in[...]
    values[...] = value_in[...]
    blocks = keys.shape[0]
    group = min(8, blocks)

    def index_of(first, count):
        shape = (count, 8, LANES)
        return (
            (first + lax.broadcasted_iota(jnp.int32, shape, 0)) * (8 * LANES)
            + lax.broadcasted_iota(jnp.int32, shape, 1) * LANES
            + lax.broadcasted_iota(jnp.int32, shape, 2)
        )

    def far(distance, span):
        for first in range(0, blocks, 2 * distance):
            for start in range(first, first + distance, group):
                count = min(group, distance)
                low, high = pl.ds(start, count), pl.ds(start + distance, count)
                a, b, x, y = keys[low], keys[high], values[low], values[high]
                up = (index_of(start, count) & span) == 0
                swap = (up & (a > b)) | (jnp.logical_not(up) & (b > a))
                keys[low] = jnp.where(swap, b, a)
                keys[high] = jnp.where(swap, a, b)
                values[low] = jnp.where(swap, y, x)
                values[high] = jnp.where(swap, x, y)

    def near(axis, shift, bit, span):
        size = 8 if axis == 1 else LANES
        for start in range(0, blocks, group):
            part = pl.ds(start, group)
            a, x = keys[part], values[part]
            index = index_of(start, group)
            upper = (index & bit) != 0
            keep_min = ((index & span) == 0) != upper

            def partner(v):
                return jnp.where(
                    upper, pltpu.roll(v, shift, axis), pltpu.roll(v, size - shift, axis)
                )

            b, y = partner(a), partner(x)
            swap = (keep_min & (b < a)) | (jnp.logical_not(keep_min) & (b > a))
            keys[part] = jnp.where(swap, b, a)
            values[part] = jnp.where(swap, y, x)

    @pl.loop(0, bits)
    def _(phase):
        span = jnp.left_shift(jnp.int32(1), phase + 1)
        for q in reversed(range(bits)):

            @pl.when(q <= phase)
            def _():
                bit = 1 << q
                if bit >= 8 * LANES:
                    far(bit // (8 * LANES), span)
                elif bit >= LANES:
                    near(1, bit // LANES, bit, span)
                else:
                    near(2, bit, bit, span)


def sort_probes(keys, values):
    count = keys.shape[0]
    bits = log2_of(count)
    shape = (count // (8 * LANES), 8, LANES)
    spec = pl.BlockSpec(memory_space=pltpu.VMEM)
    keys, values = pl.pallas_call(
        functools.partial(sort_kernel, bits),
        out_shape=(
            jax.ShapeDtypeStruct(shape, jnp.int32),
            jax.ShapeDtypeStruct(shape, jnp.float32),
        ),
        in_specs=[spec, spec],
        out_specs=(spec, spec),
        cost_estimate=pl.CostEstimate(
            flops=count * 2000, bytes_accessed=count * 16, transcendentals=0
        ),
        name="sort_probes",
    )(keys.reshape(shape), values.reshape(shape))
    return keys.reshape(count // LANES, LANES), values.reshape(count // LANES, LANES)


def bins_kernel(planes, row_bits, col_bits, starts, keys, values, out):
    rows, cols = 1 << row_bits, 1 << col_bits
    blocks = keys.shape[0]
    span = 2 * LANES
    number = pl.program_id(0)
    bucket = jnp.where(number < planes - 4, planes + 2 + number, number - (planes - 4) + 3)
    first, last = starts[bucket], starts[bucket + 1]
    block = first // LANES
    lane_rows = lax.broadcasted_iota(jnp.int32, (rows, span), 0)
    lane_cols = lax.broadcasted_iota(jnp.int32, (cols, span), 0)

    def partial(index):
        at = [jnp.minimum(index + i, blocks - 1) for i in range(2)]
        own = [
            jnp.right_shift(keys[pl.ds(at[i], 1), :], col_bits + row_bits)
            == jnp.where(index + i < blocks, bucket, -1)
            for i in range(2)
        ]
        key = [keys[pl.ds(i, 1), :] for i in at]
        row = jnp.concatenate(
            [
                jnp.where(mine, jnp.right_shift(k, col_bits) & (rows - 1), -1)
                for mine, k in zip(own, key)
            ],
            axis=1,
        )
        col = jnp.concatenate(key, axis=1) & (cols - 1)
        value = jnp.concatenate([values[pl.ds(i, 1), :] for i in at], axis=1)
        high = value.astype(jnp.bfloat16).astype(jnp.float32)
        rest = value - high
        row_hot = jnp.where(lane_rows == row, 1.0, 0.0).astype(jnp.bfloat16)
        col_hit = lane_cols == col

        def hot(v):
            return jnp.where(col_hit, v, 0.0).astype(jnp.bfloat16)

        def product(a, b):
            return lax.dot_general(
                a, b, (((1,), (1,)), ((), ())), preferred_element_type=jnp.float32
            )

        return product(row_hot, hot(1.0)), product(
            jnp.concatenate([row_hot, row_hot], axis=1),
            jnp.concatenate([hot(high), hot(rest)], axis=1),
        )

    out[0, 0], out[0, 1] = partial(block)

    @pl.loop(1, jnp.maximum((last + span - 1 - block * LANES) // span, 1))
    def _(turn):
        count, total = partial(block + 2 * turn)
        out[0, 0] += count
        out[0, 1] += total


def bins(starts, keys, values, planes, rows, cols):
    total = 2 * planes - 10
    vmem = pl.BlockSpec(memory_space=pltpu.VMEM)
    return pl.pallas_call(
        functools.partial(bins_kernel, planes, log2_of(rows), log2_of(cols)),
        grid=(total,),
        out_shape=jax.ShapeDtypeStruct((total, 2, rows, cols), jnp.float32),
        in_specs=[pl.BlockSpec(memory_space=pltpu.SMEM), vmem, vmem],
        out_specs=pl.BlockSpec((1, 2, rows, cols), lambda i: (i, 0, 0, 0)),
        compiler_params=pltpu.CompilerParams(vmem_limit_bytes=24 * 1024 * 1024),
        cost_estimate=pl.CostEstimate(
            flops=total * rows * cols * 1536, bytes_accessed=total * rows * cols * 8, transcendentals=0
        ),
        name="bins",
    )(starts, keys, values)


def field_kernel(
    place,
    velocity,
    profile,
    rate_ref,
    rate_low,
    rate_high,
    init_ref,
    init_low,
    init_high,
    probe_fields,
    out,
    kappa,
    state0,
    state1,
    adjoint2,
    adjoint1,
    face_z,
    face_x,
    face_y,
    wind,
    sums,
    injects,
    sems,
    probe_sems,
):
    slab, rows, cols = rate_ref.shape
    planes = slab + 2 * HALO

    def fetch(number):
        slot = lax.rem(number, AHEAD)
        return pltpu.make_async_copy(
            probe_fields.at[number], injects.at[slot], probe_sems.at[slot]
        )

    copies = []
    for number, (own, low, high, target) in enumerate(
        ((rate_ref, rate_low, rate_high, kappa), (init_ref, init_low, init_high, state0))
    ):
        for part, (source, first, count) in enumerate(
            ((own, HALO, slab), (low, 0, HALO), (high, HALO + slab, HALO))
        ):
            copy = pltpu.make_async_copy(
                source, target.at[pl.ds(first, count)], sems.at[3 * number + part]
            )
            copy.start()
            copies.append(copy)
    for number in range(AHEAD):
        fetch(number).start()
    for copy in copies:
        copy.wait()

    starting = range(0, rows, STRIP)
    half = 0.5 * TIME_STEP

    def window(ref, z, r, after=True):
        pieces = [ref[z, pl.ds((r - 8) % rows, 8), :], ref[z, pl.ds(r, STRIP), :]]
        if after:
            pieces.append(ref[z, pl.ds((r + STRIP) % rows, 8), :])
        return jnp.concatenate(pieces, axis=0)

    def steps_down(wide):
        return (pltpu.roll(wide, wide.shape[0] - 1, 0) - wide)[: STRIP + 8]

    def with_previous(flux):
        return flux[8:], pltpu.roll(flux, 1, 0)[8:]

    def ahead(v):
        return pltpu.roll(v, cols - 1, 1)

    def behind(v):
        return pltpu.roll(v, 1, 1)

    @pl.loop(0, planes)
    def _(z):
        for r in starting:
            part = pl.ds(r, STRIP)
            kappa[z, part, :] = jnp.exp(kappa[z, part, :])

    @pl.loop(0, planes - 1)
    def _(z):
        for r in starting:
            part = pl.ds(r, STRIP)
            wide = window(kappa, z, r)
            k = wide[8 : 8 + STRIP]
            face_z[z, part, :] = half * (k + kappa[z + 1, part, :])
            face_x[z, part, :] = half * (k + pltpu.roll(wide, STRIP + 15, 0)[8 : 8 + STRIP])
            face_y[z, part, :] = half * (k + ahead(k))

    for r in starting:
        part = pl.ds(r, STRIP)
        wind[part, :] = TIME_STEP * velocity[part, :]

    def stepped(ref, z, r, forward):
        part = pl.ds(r, STRIP)
        wide = window(ref, z, r)
        v = wide[8 : 8 + STRIP]
        upper, lower = face_z[z, part, :], face_z[z - 1, part, :]
        if forward:
            lower = lower + wind[part, :]
        else:
            upper = upper + wind[part, :]
        total = upper * (ref[z + 1, part, :] - v) - lower * (v - ref[z - 1, part, :])
        flux, previous = with_previous(window(face_x, z, r, False) * steps_down(wide))
        total = total + (flux - previous)
        flux = face_y[z, part, :] * (ahead(v) - v)
        return v + (total + (flux - behind(flux)))

    source_plane = place[0]

    def forward(ref, z, r):
        scale = jnp.where(z == source_plane, jnp.float32(TIME_STEP), jnp.float32(0.0))
        return stepped(ref, z, r, True) + scale * profile[pl.ds(r, STRIP), :]

    @pl.loop(1, planes - 1)
    def _(z):
        for r in starting:
            state1[z, pl.ds(r, STRIP), :] = forward(state0, z, r)

    def probes(number):
        fetch(number).wait()
        return lax.rem(number, AHEAD)

    def refill(number):
        @pl.when(number + AHEAD < probe_fields.shape[0])
        def _():
            fetch(number + AHEAD).start()

    @pl.loop(2, planes - 2)
    def _(z):
        number = z - 2
        slot = probes(number)
        for r in starting:
            part = pl.ds(r, STRIP)
            count, total = injects[slot, 0, part, :], injects[slot, 1, part, :]
            adjoint2[z, part, :] = count * forward(state1, z, r) - total
        refill(number)

    @pl.loop(3, planes - 3)
    def _(z):
        number = planes - 4 + z - 3
        slot = probes(number)
        for r in starting:
            part = pl.ds(r, STRIP)
            inject = injects[slot, 0, part, :] * state1[z, part, :] - injects[slot, 1, part, :]
            adjoint1[z, part, :] = stepped(adjoint2, z, r, False) + inject
        refill(number)

    fields = ((state1, adjoint2), (state0, adjoint1))

    def upward(z, part):
        return sum(
            (state[z + 1, part, :] - state[z, part, :])
            * (adjoint[z + 1, part, :] - adjoint[z, part, :])
            for state, adjoint in fields
        )

    def level(z, r):
        wide = [(window(state, z, r), window(adjoint, z, r)) for state, adjoint in fields]
        flux, previous = with_previous(sum(steps_down(c) * steps_down(m) for c, m in wide))
        total = flux + previous
        inner = [(c[8 : 8 + STRIP], m[8 : 8 + STRIP]) for c, m in wide]
        flux = sum((ahead(c) - c) * (ahead(m) - m) for c, m in inner)
        return total + (flux + behind(flux))

    def pool(length):
        shape = (length, length // R)
        fine = lax.broadcasted_iota(jnp.int32, shape, 0)
        coarse = lax.broadcasted_iota(jnp.int32, shape, 1)
        return jnp.where((fine >= coarse * R) & (fine < coarse * R + R), 1.0, 0.0)

    def exact(a, b, dims):
        return lax.dot_general(
            a,
            b,
            (dims, ((), ())),
            precision=lax.Precision.HIGHEST,
            preferred_element_type=jnp.float32,
        )

    @pl.loop(0, slab // R)
    def _(number):
        for r in starting:
            part = pl.ds(r, STRIP)
            both = jnp.zeros((STRIP, cols), jnp.float32)
            below = upward(HALO + number * R - 1, part)
            for layer in range(R):
                z = HALO + number * R + layer
                above = upward(z, part)
                both = both + kappa[z, part, :] * (level(z, r) + (below + above))
                below = above
            sums[part, :] = (-half) * both
        narrow = exact(sums[...], pool(cols), ((1,), (0,)))
        out[number] = exact(pool(rows), narrow, ((0,), (0,)))


def fields(place, velocity, profile, rates, inits, probe_fields):
    slab, rows, cols = rates[0].shape
    planes = slab + 2 * HALO
    smem = pl.BlockSpec(memory_space=pltpu.SMEM)
    vmem = pl.BlockSpec(memory_space=pltpu.VMEM)
    hbm = pl.BlockSpec(memory_space=pl.ANY)
    field = pltpu.VMEM((planes, rows, cols), jnp.float32)
    plane = pltpu.VMEM((rows, cols), jnp.float32)
    return pl.pallas_call(
        field_kernel,
        out_shape=jax.ShapeDtypeStruct((slab // R, rows // R, cols // R), jnp.float32),
        in_specs=[smem] + [vmem] * 2 + [hbm] * 7,
        out_specs=vmem,
        scratch_shapes=[field] * 8
        + [plane] * 2
        + [
            pltpu.VMEM((AHEAD, 2, rows, cols), jnp.float32),
            pltpu.SemaphoreType.DMA((6,)),
            pltpu.SemaphoreType.DMA((AHEAD,)),
        ],
        compiler_params=pltpu.CompilerParams(vmem_limit_bytes=60 * 1024 * 1024),
        cost_estimate=pl.CostEstimate(
            flops=planes * rows * cols * 200,
            bytes_accessed=planes * rows * cols * 8,
            transcendentals=planes * rows * cols,
        ),
        name="fields",
    )(place, velocity, profile, *rates, *inits, probe_fields)


def tail_kernel(
    domains,
    tracers,
    coarse,
    weights,
    x_table,
    y_table,
    z_table,
    out,
    send_sum,
    recv_sum,
    send_z,
    recv_z,
    send_back,
    recv_back,
    send_x,
    recv_x,
    sum_sems,
    z_sems,
    back_sems,
    x_sems,
):
    depth, x_size, y_size = coarse.shape
    y_share, x_share = y_size // tracers, x_size // tracers
    y_own = y_share // domains
    z_size = depth * domains
    tracer, domain = lax.axis_index("tracer"), lax.axis_index("domain")

    barrier = pltpu.get_barrier_semaphore()
    for axis, me, count in (("tracer", tracer, tracers), ("domain", domain, domains)):
        for i in range(1, count):
            pl.semaphore_signal(
                barrier,
                inc=1,
                device_id={axis: lax.rem(me + i, count)},
                device_id_type=pl.DeviceIdType.MESH,
            )
    pl.semaphore_wait(barrier, tracers + domains - 2)

    def exact(a, b, dims):
        return lax.dot_general(
            a,
            b,
            (dims, ((), ())),
            precision=lax.Precision.HIGHEST,
            preferred_element_type=jnp.float32,
        )

    def exchange(axis, me, count, source, target, sems):
        copies = []
        for i in range(1, count):
            peer = lax.rem(me + i, count)
            copy = pltpu.make_async_remote_copy(
                src_ref=source(peer),
                dst_ref=target(i, me),
                send_sem=sems.at[0, i],
                recv_sem=sems.at[1, i],
                device_id={axis: peer},
                device_id_type=pl.DeviceIdType.MESH,
            )
            copy.start()
            copies.append(copy)
        return copies

    spectral = exact(y_table[...], coarse[...].reshape(depth * x_size, y_size), ((1,), (1,)))
    for block in range(tracers):
        send_sum[block] = spectral[block * y_share : (block + 1) * y_share]
    first = exchange(
        "tracer",
        tracer,
        tracers,
        lambda peer: send_sum.at[peer],
        lambda i, me: recv_sum.at[i],
        sum_sems,
    )
    total = send_sum[tracer]
    for i, copy in enumerate(first):
        copy.wait_recv()
        total = total + recv_sum[i + 1]

    for z in range(depth):
        send_z[:, z, :] = exact(
            total[:, z * x_size : (z + 1) * x_size], x_table[...], ((1,), (0,))
        )
    second = exchange(
        "domain",
        domain,
        domains,
        lambda peer: send_z.at[pl.ds(peer * y_own, y_own)],
        lambda i, me: recv_z.at[me],
        z_sems,
    )
    recv_z[domain] = send_z[pl.ds(domain * y_own, y_own)]
    for copy in second:
        copy.wait_recv()

    for k in range(y_own):
        column = recv_z[:, k].reshape(z_size, x_size)
        column = exact(z_table[...], column, ((1,), (0,))) * weights[k]
        column = exact(z_table[...], column, ((1,), (0,)))
        send_back[:, k] = column.reshape(domains, depth, x_size)
    third = exchange(
        "domain",
        domain,
        domains,
        lambda peer: send_back.at[peer],
        lambda i, me: recv_back.at[pl.ds(me * y_own, y_own)],
        back_sems,
    )
    recv_back[pl.ds(domain * y_own, y_own)] = send_back[domain]
    for copy in third:
        copy.wait_recv()

    spectral = jnp.concatenate([recv_back[:, z, :] for z in range(depth)], axis=0)
    spectral = exact(x_table[...], spectral, ((1,), (1,)))
    for block in range(tracers):
        send_x[block] = spectral[block * x_share : (block + 1) * x_share]
    fourth = exchange(
        "tracer",
        tracer,
        tracers,
        lambda peer: send_x.at[peer],
        lambda i, me: recv_x.at[me],
        x_sems,
    )
    recv_x[tracer] = send_x[tracer]
    for copy in fourth:
        copy.wait_recv()

    for z in range(depth):
        lanes = slice(z * y_share, (z + 1) * y_share)
        row = jnp.concatenate([recv_x[i][:, lanes] for i in range(tracers)], axis=1)
        out[z] = exact(row, y_table[...], ((1,), (0,)))
    for copy in first + second + third + fourth:
        copy.wait_send()


def filtered(coarse, weights, x_table, y_table, z_table):
    depth, x_size, y_size = coarse.shape
    domains, tracers = lax.axis_size("domain"), lax.axis_size("tracer")
    y_share, x_share = y_size // tracers, x_size // tracers
    y_own = y_share // domains
    vmem = pl.BlockSpec(memory_space=pltpu.VMEM)

    def buffer(*shape):
        return pltpu.VMEM(shape, jnp.float32)

    def sems(count):
        return pltpu.SemaphoreType.DMA((2, count))

    return pl.pallas_call(
        functools.partial(tail_kernel, domains, tracers),
        out_shape=jax.ShapeDtypeStruct((depth, x_share, y_size), jnp.float32),
        in_specs=[vmem] * 5,
        out_specs=vmem,
        scratch_shapes=[
            buffer(tracers, y_share, depth * x_size),
            buffer(tracers, y_share, depth * x_size),
            buffer(y_share, depth, x_size),
            buffer(domains, y_own, depth, x_size),
            buffer(domains, y_own, depth, x_size),
            buffer(y_share, depth, x_size),
            buffer(tracers, x_share, depth * y_share),
            buffer(tracers, x_share, depth * y_share),
            sems(tracers),
            sems(domains),
            sems(domains),
            sems(tracers),
        ],
        compiler_params=pltpu.CompilerParams(
            collective_id=1, has_side_effects=True, vmem_limit_bytes=24 * 1024 * 1024
        ),
        cost_estimate=pl.CostEstimate(
            flops=coarse.size * 3000, bytes_accessed=coarse.size * 8, transcendentals=0
        ),
        name="filtered",
    )(coarse, weights, x_table, y_table, z_table)


def halos(array, axis, width):
    count, length = lax.axis_size(axis), array.shape[0]
    up = [(i, (i + 1) % count) for i in range(count)]
    down = [(j, i) for i, j in up]
    before = lax.ppermute(array[length - width :], axis, up)
    after = lax.ppermute(array[:width], axis, down)
    return array, before, after


def hartley(length, first_row, count):
    indices = first_row + lax.iota(jnp.int32, count)
    phases = indices[:, None] * lax.iota(jnp.int32, length)[None, :] % length
    angles = 2.0 * math.pi / length * phases.astype(jnp.float32)
    return jnp.cos(angles) + jnp.sin(angles)


def symbol_part(length, first_row, count):
    indices = (first_row + lax.iota(jnp.int32, count)) % length
    angles = 2.0 * math.pi / length * indices.astype(jnp.float32)
    return 2.0 - 2.0 * jnp.cos(angles)


def local(log_rate, velocity, initial, profile, plane, depth, row, column, step_of, observed):
    slab, rows, cols = log_rate.shape
    domains, tracers = lax.axis_size("domain"), lax.axis_size("tracer")
    full = slab * domains
    planes = slab + 2 * HALO
    first = lax.axis_index("domain") * slab - HALO
    rates = halos(log_rate, "domain", HALO)
    inits = halos(initial[0], "domain", HALO)

    layer = (depth[0] - first + full) % full
    bucket = jnp.where(layer < planes, (step_of[0] - 1) * planes + layer, STEPS * planes)
    keys = bucket * (rows * cols) + row[0] * cols + column[0]
    edges = lax.iota(jnp.int32, STEPS * planes + 1)
    starts = jnp.sum((bucket[None, :] < edges[:, None]).astype(jnp.int32), axis=1)
    keys, values = sort_probes(keys, observed[0])
    place = (plane - first + full) % full

    probe_fields = bins(starts, keys, values, planes, rows, cols)
    coarse = fields(place, velocity, profile[0], rates, inits, probe_fields)

    x_size, y_size, z_size = rows // R, cols // R, full // R
    y_own = y_size // (tracers * domains)
    own_first = (lax.axis_index("tracer") * domains + lax.axis_index("domain")) * y_own
    lam = (
        symbol_part(y_size, own_first, y_own)[:, None, None]
        + symbol_part(z_size, 0, z_size)[None, :, None]
        + symbol_part(x_size, 0, x_size)[None, None, :]
    )
    factor = 1.0 + PRIOR_RANGE * lam
    weights = 1.0 / (factor * factor) / (x_size * y_size * z_size)
    tables = [hartley(size, 0, size) for size in (x_size, y_size, z_size)]
    return filtered(coarse, weights, *tables)


def solution(mesh):
    return jax.shard_map(
        local,
        mesh=mesh,
        in_specs=(
            P("domain", None, None),
            P(),
            P("tracer", "domain", None, None),
            P("tracer", None, None),
            P("tracer"),
            P("tracer", None),
            P("tracer", None),
            P("tracer", None),
            P("tracer", None),
            P("tracer", None),
        ),
        out_specs=P("domain", "tracer", None),
        check_vma=False,
    )
```

```python
import functools
import math

import jax
import jax.numpy as jnp
from jax import lax
from jax.experimental import pallas as pl
from jax.experimental.pallas import tpu as pltpu
from jax.sharding import PartitionSpec as P

R = 2
STEPS = 2
HALO = 2 * STEPS
STRIP = 64
LANES = 128
AHEAD = 4
SORT_BITS = 15
BLOCKS = (1 << SORT_BITS) // (8 * LANES)
VMEM_LIMIT = 60 * 1024 * 1024

TIME_STEP = 0.14
PRIOR_RANGE = 4.0


def log2_of(size):
    bits = size.bit_length() - 1
    assert size == 1 << bits
    return bits


def sort_kernel(
    planes,
    full,
    shift_row,
    shift_bucket,
    first,
    depth,
    row,
    column,
    step,
    observed,
    keys_out,
    values_out,
    keys,
    values,
):
    layer = depth[...] - first[0]
    layer = jnp.where(layer < 0, layer + full, layer)
    layer = jnp.where(layer >= full, layer - full, layer)
    bucket = jnp.where(layer < planes, (step[...] - 1) * planes + layer, STEPS * planes)
    keys[...] = (
        jnp.left_shift(bucket, shift_bucket) | jnp.left_shift(row[...], shift_row) | column[...]
    )
    values[...] = observed[...]
    group = 8

    def index_of(start, count):
        shape = (count, 8, LANES)
        major = start + lax.broadcasted_iota(jnp.int32, shape, 0)
        return (
            (major & 15)
            | jnp.left_shift(lax.broadcasted_iota(jnp.int32, shape, 1), 4)
            | jnp.left_shift(jnp.right_shift(major, 4), 7)
            | jnp.left_shift(lax.broadcasted_iota(jnp.int32, shape, 2), 8)
        )

    def far(distance, span):
        for begin in range(0, BLOCKS, 2 * distance):
            for start in range(begin, begin + distance, group):
                count = min(group, distance)
                low, high = pl.ds(start, count), pl.ds(start + distance, count)
                a, b, x, y = keys[low], keys[high], values[low], values[high]
                up = (index_of(start, count) & span) == 0
                swap = (up & (a > b)) | (jnp.logical_not(up) & (b > a))
                keys[low] = jnp.where(swap, b, a)
                keys[high] = jnp.where(swap, a, b)
                values[low] = jnp.where(swap, y, x)
                values[high] = jnp.where(swap, x, y)

    def near(axis, shift, bit, span):
        size = 8 if axis == 1 else LANES
        for start in range(0, BLOCKS, group):
            part = pl.ds(start, group)
            a, x = keys[part], values[part]
            index = index_of(start, group)
            upper = (index & bit) != 0
            keep_min = ((index & span) == 0) != upper

            def partner(v):
                return jnp.where(
                    upper, pltpu.roll(v, shift, axis), pltpu.roll(v, size - shift, axis)
                )

            b, y = partner(a), partner(x)
            swap = (keep_min & (b < a)) | (jnp.logical_not(keep_min) & (b > a))
            keys[part] = jnp.where(swap, b, a)
            values[part] = jnp.where(swap, y, x)

    @pl.loop(0, SORT_BITS)
    def _(phase):
        span = jnp.left_shift(jnp.int32(1), phase + 1)
        for q in reversed(range(SORT_BITS)):

            @pl.when(q <= phase)
            def _():
                bit = 1 << q
                if q < 4:
                    far(bit, span)
                elif q == 7:
                    far(16, span)
                elif q < 7:
                    near(1, bit >> 4, bit, span)
                else:
                    near(2, bit >> 8, bit, span)

    for half in range(2):
        part = pl.ds(16 * half, 16)
        keys_out[half] = keys[part].reshape(LANES, LANES).T
        values_out[half] = values[part].reshape(LANES, LANES).T


def sort_probes(first, planes, full, rows, cols, probes):
    shape = (BLOCKS, 8, LANES)
    assert probes[0].size == 1 << SORT_BITS
    vmem = pl.BlockSpec(memory_space=pltpu.VMEM)
    sizes = (2, LANES, LANES)
    return pl.pallas_call(
        functools.partial(
            sort_kernel, planes, full, log2_of(cols), log2_of(rows) + log2_of(cols)
        ),
        out_shape=(
            jax.ShapeDtypeStruct(sizes, jnp.int32),
            jax.ShapeDtypeStruct(sizes, jnp.float32),
        ),
        in_specs=[pl.BlockSpec(memory_space=pltpu.SMEM)] + [vmem] * 5,
        out_specs=(vmem, vmem),
        scratch_shapes=[pltpu.VMEM(shape, jnp.int32), pltpu.VMEM(shape, jnp.float32)],
        compiler_params=pltpu.CompilerParams(vmem_limit_bytes=VMEM_LIMIT),
        cost_estimate=pl.CostEstimate(
            flops=2000 << SORT_BITS, bytes_accessed=28 << SORT_BITS, transcendentals=0
        ),
        name="sort_probes",
    )(first, *[array.reshape(shape) for array in probes])


def bins_kernel(planes, row_bits, col_bits, starts, keys, values, out):
    rows, cols = 1 << row_bits, 1 << col_bits
    blocks = 2 * LANES
    span = 2 * LANES
    number = pl.program_id(0)
    bucket = jnp.where(number < planes - 4, planes + 2 + number, number - (planes - 4) + 3)
    first, last = starts[bucket], starts[bucket + 1]
    block = first // LANES
    lane_rows = lax.broadcasted_iota(jnp.int32, (rows, span), 0)
    lane_cols = lax.broadcasted_iota(jnp.int32, (cols, span), 0)

    def chunk(ref, index):
        return ref[index & 1, pl.ds(jnp.right_shift(index, 1), 1), :]

    def partial(index):
        at = [jnp.minimum(index + i, blocks - 1) for i in range(2)]
        own = [
            jnp.right_shift(chunk(keys, at[i]), col_bits + row_bits)
            == jnp.where(index + i < blocks, bucket, -1)
            for i in range(2)
        ]
        key = [chunk(keys, i) for i in at]
        row = jnp.concatenate(
            [
                jnp.where(mine, jnp.right_shift(k, col_bits) & (rows - 1), -1)
                for mine, k in zip(own, key)
            ],
            axis=1,
        )
        col = jnp.concatenate(key, axis=1) & (cols - 1)
        value = jnp.concatenate([chunk(values, i) for i in at], axis=1)
        high = value.astype(jnp.bfloat16).astype(jnp.float32)
        rest = value - high
        row_hot = jnp.where(lane_rows == row, 1.0, 0.0).astype(jnp.bfloat16)
        col_hit = lane_cols == col

        def hot(v):
            return jnp.where(col_hit, v, 0.0).astype(jnp.bfloat16)

        def product(a, b):
            return lax.dot_general(
                a, b, (((1,), (1,)), ((), ())), preferred_element_type=jnp.float32
            )

        return product(row_hot, hot(1.0)), product(
            jnp.concatenate([row_hot, row_hot], axis=1),
            jnp.concatenate([hot(high), hot(rest)], axis=1),
        )

    out[0, 0], out[0, 1] = partial(block)

    @pl.loop(1, jnp.maximum((last + span - 1 - block * LANES) // span, 1))
    def _(turn):
        count, total = partial(block + 2 * turn)
        out[0, 0] += count
        out[0, 1] += total


def bins(starts, keys, values, planes, rows, cols):
    total = 2 * planes - 10
    vmem = pl.BlockSpec(memory_space=pltpu.VMEM)
    return pl.pallas_call(
        functools.partial(bins_kernel, planes, log2_of(rows), log2_of(cols)),
        grid=(total,),
        out_shape=jax.ShapeDtypeStruct((total, 2, rows, cols), jnp.float32),
        in_specs=[pl.BlockSpec(memory_space=pltpu.SMEM), vmem, vmem],
        out_specs=pl.BlockSpec((1, 2, rows, cols), lambda i: (i, 0, 0, 0)),
        compiler_params=pltpu.CompilerParams(vmem_limit_bytes=VMEM_LIMIT),
        cost_estimate=pl.CostEstimate(
            flops=total * rows * cols * 1536, bytes_accessed=total * rows * cols * 8, transcendentals=0
        ),
        name="bins",
    )(starts, keys, values)


def field_kernel(
    place,
    velocity,
    profile,
    rate_ref,
    init_ref,
    below,
    above,
    probe_fields,
    out,
    kappa,
    state0,
    state1,
    adjoint2,
    adjoint1,
    face_z,
    face_x,
    face_y,
    wind,
    sums,
    injects,
    sems,
    probe_sems,
):
    slab, rows, cols = rate_ref.shape
    planes = slab + 2 * HALO

    def fetch(number):
        slot = lax.rem(number, AHEAD)
        return pltpu.make_async_copy(
            probe_fields.at[number], injects.at[slot], probe_sems.at[slot]
        )

    copies = []
    for number, (own, target) in enumerate(((rate_ref, kappa), (init_ref, state0))):
        for part, (source, first, count) in enumerate(
            (
                (own, HALO, slab),
                (below.at[number], 0, HALO),
                (above.at[number], HALO + slab, HALO),
            )
        ):
            copy = pltpu.make_async_copy(
                source, target.at[pl.ds(first, count)], sems.at[3 * number + part]
            )
            copy.start()
            copies.append(copy)
    for number in range(AHEAD):
        fetch(number).start()
    for copy in copies:
        copy.wait()

    starting = range(0, rows, STRIP)
    half = 0.5 * TIME_STEP

    def window(ref, z, r, after=True):
        pieces = [ref[z, pl.ds((r - 8) % rows, 8), :], ref[z, pl.ds(r, STRIP), :]]
        if after:
            pieces.append(ref[z, pl.ds((r + STRIP) % rows, 8), :])
        return jnp.concatenate(pieces, axis=0)

    def steps_down(wide):
        return (pltpu.roll(wide, wide.shape[0] - 1, 0) - wide)[: STRIP + 8]

    def with_previous(flux):
        return flux[8:], pltpu.roll(flux, 1, 0)[8:]

    def ahead(v):
        return pltpu.roll(v, cols - 1, 1)

    def behind(v):
        return pltpu.roll(v, 1, 1)

    @pl.loop(0, planes)
    def _(z):
        for r in starting:
            part = pl.ds(r, STRIP)
            kappa[z, part, :] = jnp.exp(kappa[z, part, :])

    @pl.loop(0, planes - 1)
    def _(z):
        for r in starting:
            part = pl.ds(r, STRIP)
            wide = window(kappa, z, r)
            k = wide[8 : 8 + STRIP]
            face_z[z, part, :] = half * (k + kappa[z + 1, part, :])
            face_x[z, part, :] = half * (k + pltpu.roll(wide, STRIP + 15, 0)[8 : 8 + STRIP])
            face_y[z, part, :] = half * (k + ahead(k))

    for r in starting:
        part = pl.ds(r, STRIP)
        wind[part, :] = TIME_STEP * velocity[part, :]

    def stepped(ref, z, r, forward):
        part = pl.ds(r, STRIP)
        wide = window(ref, z, r)
        v = wide[8 : 8 + STRIP]
        upper, lower = face_z[z, part, :], face_z[z - 1, part, :]
        if forward:
            lower = lower + wind[part, :]
        else:
            upper = upper + wind[part, :]
        total = upper * (ref[z + 1, part, :] - v) - lower * (v - ref[z - 1, part, :])
        flux, previous = with_previous(window(face_x, z, r, False) * steps_down(wide))
        total = total + (flux - previous)
        flux = face_y[z, part, :] * (ahead(v) - v)
        return v + (total + (flux - behind(flux)))

    source_plane = place[0]

    def forward(ref, z, r):
        scale = jnp.where(z == source_plane, jnp.float32(TIME_STEP), jnp.float32(0.0))
        return stepped(ref, z, r, True) + scale * profile[pl.ds(r, STRIP), :]

    @pl.loop(1, planes - 1)
    def _(z):
        for r in starting:
            state1[z, pl.ds(r, STRIP), :] = forward(state0, z, r)

    def probes(number):
        fetch(number).wait()
        return lax.rem(number, AHEAD)

    def refill(number):
        @pl.when(number + AHEAD < probe_fields.shape[0])
        def _():
            fetch(number + AHEAD).start()

    @pl.loop(2, planes - 2)
    def _(z):
        number = z - 2
        slot = probes(number)
        for r in starting:
            part = pl.ds(r, STRIP)
            count, total = injects[slot, 0, part, :], injects[slot, 1, part, :]
            adjoint2[z, part, :] = count * forward(state1, z, r) - total
        refill(number)

    @pl.loop(3, planes - 3)
    def _(z):
        number = planes - 4 + z - 3
        slot = probes(number)
        for r in starting:
            part = pl.ds(r, STRIP)
            inject = injects[slot, 0, part, :] * state1[z, part, :] - injects[slot, 1, part, :]
            adjoint1[z, part, :] = stepped(adjoint2, z, r, False) + inject
        refill(number)

    fields = ((state1, adjoint2), (state0, adjoint1))

    def upward(z, part):
        return sum(
            (state[z + 1, part, :] - state[z, part, :])
            * (adjoint[z + 1, part, :] - adjoint[z, part, :])
            for state, adjoint in fields
        )

    def level(z, r):
        wide = [(window(state, z, r), window(adjoint, z, r)) for state, adjoint in fields]
        flux, previous = with_previous(sum(steps_down(c) * steps_down(m) for c, m in wide))
        total = flux + previous
        inner = [(c[8 : 8 + STRIP], m[8 : 8 + STRIP]) for c, m in wide]
        flux = sum((ahead(c) - c) * (ahead(m) - m) for c, m in inner)
        return total + (flux + behind(flux))

    def pool(length):
        shape = (length, length // R)
        fine = lax.broadcasted_iota(jnp.int32, shape, 0)
        coarse = lax.broadcasted_iota(jnp.int32, shape, 1)
        return jnp.where((fine >= coarse * R) & (fine < coarse * R + R), 1.0, 0.0)

    def exact(a, b, dims):
        return lax.dot_general(
            a,
            b,
            (dims, ((), ())),
            precision=lax.Precision.HIGHEST,
            preferred_element_type=jnp.float32,
        )

    @pl.loop(0, slab // R)
    def _(number):
        for r in starting:
            part = pl.ds(r, STRIP)
            both = jnp.zeros((STRIP, cols), jnp.float32)
            below = upward(HALO + number * R - 1, part)
            for layer in range(R):
                z = HALO + number * R + layer
                above = upward(z, part)
                both = both + kappa[z, part, :] * (level(z, r) + (below + above))
                below = above
            sums[part, :] = (-half) * both
        narrow = exact(sums[...], pool(cols), ((1,), (0,)))
        out[number] = exact(pool(rows), narrow, ((0,), (0,)))


def fields(place, velocity, profile, rate, init, below, above, probe_fields):
    slab, rows, cols = rate.shape
    planes = slab + 2 * HALO
    smem = pl.BlockSpec(memory_space=pltpu.SMEM)
    vmem = pl.BlockSpec(memory_space=pltpu.VMEM)
    anywhere = pl.BlockSpec(memory_space=pl.ANY)
    field = pltpu.VMEM((planes, rows, cols), jnp.float32)
    plane = pltpu.VMEM((rows, cols), jnp.float32)
    return pl.pallas_call(
        field_kernel,
        out_shape=jax.ShapeDtypeStruct((slab // R, rows // R, cols // R), jnp.float32),
        in_specs=[smem] + [vmem] * 2 + [anywhere] * 5,
        out_specs=vmem,
        scratch_shapes=[field] * 8
        + [plane] * 2
        + [
            pltpu.VMEM((AHEAD, 2, rows, cols), jnp.float32),
            pltpu.SemaphoreType.DMA((6,)),
            pltpu.SemaphoreType.DMA((AHEAD,)),
        ],
        compiler_params=pltpu.CompilerParams(vmem_limit_bytes=VMEM_LIMIT),
        cost_estimate=pl.CostEstimate(
            flops=planes * rows * cols * 200,
            bytes_accessed=planes * rows * cols * 8,
            transcendentals=planes * rows * cols,
        ),
        name="fields",
    )(place, velocity, profile, rate, init, below, above, probe_fields)


def tail_kernel(
    domains,
    tracers,
    coarse,
    weights,
    x_table,
    y_table,
    z_table,
    out,
    send_sum,
    recv_sum,
    send_z,
    recv_z,
    send_back,
    recv_back,
    send_x,
    recv_x,
    sum_sems,
    z_sems,
    back_sems,
    x_sems,
):
    depth, x_size, y_size = coarse.shape
    y_share, x_share = y_size // tracers, x_size // tracers
    y_own = y_share // domains
    z_size = depth * domains
    tracer, domain = lax.axis_index("tracer"), lax.axis_index("domain")

    barrier = pltpu.get_barrier_semaphore()
    for axis, me, count in (("tracer", tracer, tracers), ("domain", domain, domains)):
        for i in range(1, count):
            pl.semaphore_signal(
                barrier,
                inc=1,
                device_id={axis: lax.rem(me + i, count)},
                device_id_type=pl.DeviceIdType.MESH,
            )
    pl.semaphore_wait(barrier, tracers + domains - 2)

    def exact(a, b, dims):
        return lax.dot_general(
            a,
            b,
            (dims, ((), ())),
            precision=lax.Precision.HIGHEST,
            preferred_element_type=jnp.float32,
        )

    def exchange(axis, me, count, source, target, sems):
        copies = []
        for i in range(1, count):
            peer = lax.rem(me + i, count)
            copy = pltpu.make_async_remote_copy(
                src_ref=source(peer),
                dst_ref=target(i, me),
                send_sem=sems.at[0, i],
                recv_sem=sems.at[1, i],
                device_id={axis: peer},
                device_id_type=pl.DeviceIdType.MESH,
            )
            copy.start()
            copies.append(copy)
        return copies

    spectral = exact(y_table[...], coarse[...].reshape(depth * x_size, y_size), ((1,), (1,)))
    for block in range(tracers):
        send_sum[block] = spectral[block * y_share : (block + 1) * y_share]
    first = exchange(
        "tracer",
        tracer,
        tracers,
        lambda peer: send_sum.at[peer],
        lambda i, me: recv_sum.at[i],
        sum_sems,
    )
    total = send_sum[tracer]
    for i, copy in enumerate(first):
        copy.wait_recv()
        total = total + recv_sum[i + 1]

    for z in range(depth):
        send_z[:, z, :] = exact(
            total[:, z * x_size : (z + 1) * x_size], x_table[...], ((1,), (0,))
        )
    second = exchange(
        "domain",
        domain,
        domains,
        lambda peer: send_z.at[pl.ds(peer * y_own, y_own)],
        lambda i, me: recv_z.at[me],
        z_sems,
    )
    recv_z[domain] = send_z[pl.ds(domain * y_own, y_own)]
    for copy in second:
        copy.wait_recv()

    for k in range(y_own):
        column = recv_z[:, k].reshape(z_size, x_size)
        column = exact(z_table[...], column, ((1,), (0,))) * weights[k]
        column = exact(z_table[...], column, ((1,), (0,)))
        send_back[:, k] = column.reshape(domains, depth, x_size)
    third = exchange(
        "domain",
        domain,
        domains,
        lambda peer: send_back.at[peer],
        lambda i, me: recv_back.at[pl.ds(me * y_own, y_own)],
        back_sems,
    )
    recv_back[pl.ds(domain * y_own, y_own)] = send_back[domain]
    for copy in third:
        copy.wait_recv()

    spectral = jnp.concatenate([recv_back[:, z, :] for z in range(depth)], axis=0)
    spectral = exact(x_table[...], spectral, ((1,), (1,)))
    for block in range(tracers):
        send_x[block] = spectral[block * x_share : (block + 1) * x_share]
    fourth = exchange(
        "tracer",
        tracer,
        tracers,
        lambda peer: send_x.at[peer],
        lambda i, me: recv_x.at[me],
        x_sems,
    )
    recv_x[tracer] = send_x[tracer]
    for copy in fourth:
        copy.wait_recv()

    for z in range(depth):
        lanes = slice(z * y_share, (z + 1) * y_share)
        row = jnp.concatenate([recv_x[i][:, lanes] for i in range(tracers)], axis=1)
        out[z] = exact(row, y_table[...], ((1,), (0,)))
    for copy in first + second + third + fourth:
        copy.wait_send()


def filtered(coarse, weights, x_table, y_table, z_table):
    depth, x_size, y_size = coarse.shape
    domains, tracers = lax.axis_size("domain"), lax.axis_size("tracer")
    y_share, x_share = y_size // tracers, x_size // tracers
    y_own = y_share // domains
    vmem = pl.BlockSpec(memory_space=pltpu.VMEM)

    def buffer(*shape):
        return pltpu.VMEM(shape, jnp.float32)

    def sems(count):
        return pltpu.SemaphoreType.DMA((2, count))

    return pl.pallas_call(
        functools.partial(tail_kernel, domains, tracers),
        out_shape=jax.ShapeDtypeStruct((depth, x_share, y_size), jnp.float32),
        in_specs=[vmem] * 5,
        out_specs=vmem,
        scratch_shapes=[
            buffer(tracers, y_share, depth * x_size),
            buffer(tracers, y_share, depth * x_size),
            buffer(y_share, depth, x_size),
            buffer(domains, y_own, depth, x_size),
            buffer(domains, y_own, depth, x_size),
            buffer(y_share, depth, x_size),
            buffer(tracers, x_share, depth * y_share),
            buffer(tracers, x_share, depth * y_share),
            sems(tracers),
            sems(domains),
            sems(domains),
            sems(tracers),
        ],
        compiler_params=pltpu.CompilerParams(
            collective_id=1, has_side_effects=True, vmem_limit_bytes=VMEM_LIMIT
        ),
        cost_estimate=pl.CostEstimate(
            flops=coarse.size * 3000, bytes_accessed=coarse.size * 8, transcendentals=0
        ),
        name="filtered",
    )(coarse, weights, x_table, y_table, z_table)


def halos(arrays, axis, width):
    count, length = lax.axis_size(axis), arrays[0].shape[0]
    up = [(i, (i + 1) % count) for i in range(count)]
    down = [(j, i) for i, j in up]
    last = jnp.stack([array[length - width :] for array in arrays])
    initial = jnp.stack([array[:width] for array in arrays])
    return lax.ppermute(last, axis, up), lax.ppermute(initial, axis, down)


def hartley(length, first_row, count):
    indices = first_row + lax.iota(jnp.int32, count)
    phases = indices[:, None] * lax.iota(jnp.int32, length)[None, :] % length
    angles = 2.0 * math.pi / length * phases.astype(jnp.float32)
    return jnp.cos(angles) + jnp.sin(angles)


def symbol_part(length, first_row, count):
    indices = (first_row + lax.iota(jnp.int32, count)) % length
    angles = 2.0 * math.pi / length * indices.astype(jnp.float32)
    return 2.0 - 2.0 * jnp.cos(angles)


def local(log_rate, velocity, initial, profile, plane, depth, row, column, step_of, observed):
    slab, rows, cols = log_rate.shape
    domains, tracers = lax.axis_size("domain"), lax.axis_size("tracer")
    full = slab * domains
    planes = slab + 2 * HALO
    first = lax.axis_index("domain") * slab - HALO
    below, above = halos((log_rate, initial[0]), "domain", HALO)

    keys, values = sort_probes(
        first.reshape(1), planes, full, rows, cols, (depth, row, column, step_of, observed)
    )
    edges = lax.iota(jnp.int32, STEPS * planes + 1) * (rows * cols)
    starts = jnp.sum((keys[None] < edges[:, None, None, None]).astype(jnp.int32), axis=(1, 2, 3))
    place = (plane - first + full) % full

    probe_fields = bins(starts, keys, values, planes, rows, cols)
    coarse = fields(place, velocity, profile[0], log_rate, initial[0], below, above, probe_fields)

    x_size, y_size, z_size = rows // R, cols // R, full // R
    y_own = y_size // (tracers * domains)
    own_first = (lax.axis_index("tracer") * domains + lax.axis_index("domain")) * y_own
    lam = (
        symbol_part(y_size, own_first, y_own)[:, None, None]
        + symbol_part(z_size, 0, z_size)[None, :, None]
        + symbol_part(x_size, 0, x_size)[None, None, :]
    )
    factor = 1.0 + PRIOR_RANGE * lam
    weights = 1.0 / (factor * factor) / (x_size * y_size * z_size)
    tables = [hartley(size, 0, size) for size in (x_size, y_size, z_size)]
    return filtered(coarse, weights, *tables)


def solution(mesh):
    return jax.shard_map(
        local,
        mesh=mesh,
        in_specs=(
            P("domain", None, None),
            P(),
            P("tracer", "domain", None, None),
            P("tracer", None, None),
            P("tracer"),
            P("tracer", None),
            P("tracer", None),
            P("tracer", None),
            P("tracer", None),
            P("tracer", None),
        ),
        out_specs=P("domain", "tracer", None),
        check_vma=False,
    )
```

```python
import functools
import math

import jax
import jax.numpy as jnp
from jax import lax
from jax.experimental import pallas as pl
from jax.experimental.pallas import tpu as pltpu
from jax.sharding import PartitionSpec as P

R = 2
STEPS = 2
HALO = 2 * STEPS
STRIP = 32
LANES = 128
AHEAD = 4
SORT_BITS = 15
BLOCKS = (1 << SORT_BITS) // (8 * LANES)
VMEM_LIMIT = 60 * 1024 * 1024

TIME_STEP = 0.14
PRIOR_RANGE = 4.0


def log2_of(size):
    bits = size.bit_length() - 1
    assert size == 1 << bits
    return bits


def sort_kernel(
    planes,
    full,
    shift_row,
    shift_bucket,
    first,
    depth,
    row,
    column,
    step,
    observed,
    keys_out,
    values_out,
    keys,
    values,
):
    layer = depth[...] - first[0]
    layer = jnp.where(layer < 0, layer + full, layer)
    layer = jnp.where(layer >= full, layer - full, layer)
    bucket = jnp.where(layer < planes, (step[...] - 1) * planes + layer, STEPS * planes)
    keys[...] = (
        jnp.left_shift(bucket, shift_bucket) | jnp.left_shift(row[...], shift_row) | column[...]
    )
    values[...] = observed[...]
    group = 8

    def index_of(start, count):
        shape = (count, 8, LANES)
        major = start + lax.broadcasted_iota(jnp.int32, shape, 0)
        return (
            (major & 15)
            | jnp.left_shift(lax.broadcasted_iota(jnp.int32, shape, 1), 4)
            | jnp.left_shift(jnp.right_shift(major, 4), 7)
            | jnp.left_shift(lax.broadcasted_iota(jnp.int32, shape, 2), 8)
        )

    def far(distance, span):
        for begin in range(0, BLOCKS, 2 * distance):
            for start in range(begin, begin + distance, group):
                count = min(group, distance)
                low, high = pl.ds(start, count), pl.ds(start + distance, count)
                a, b, x, y = keys[low], keys[high], values[low], values[high]
                up = (index_of(start, count) & span) == 0
                swap = (up & (a > b)) | (jnp.logical_not(up) & (b > a))
                keys[low] = jnp.where(swap, b, a)
                keys[high] = jnp.where(swap, a, b)
                values[low] = jnp.where(swap, y, x)
                values[high] = jnp.where(swap, x, y)

    def near(axis, shift, bit, span):
        size = 8 if axis == 1 else LANES
        for start in range(0, BLOCKS, group):
            part = pl.ds(start, group)
            a, x = keys[part], values[part]
            index = index_of(start, group)
            upper = (index & bit) != 0
            keep_min = ((index & span) == 0) != upper

            def partner(v):
                return jnp.where(
                    upper, pltpu.roll(v, shift, axis), pltpu.roll(v, size - shift, axis)
                )

            b, y = partner(a), partner(x)
            swap = (keep_min & (b < a)) | (jnp.logical_not(keep_min) & (b > a))
            keys[part] = jnp.where(swap, b, a)
            values[part] = jnp.where(swap, y, x)

    @pl.loop(0, SORT_BITS)
    def _(phase):
        span = jnp.left_shift(jnp.int32(1), phase + 1)
        for q in reversed(range(SORT_BITS)):

            @pl.when(q <= phase)
            def _():
                bit = 1 << q
                if q < 4:
                    far(bit, span)
                elif q == 7:
                    far(16, span)
                elif q < 7:
                    near(1, bit >> 4, bit, span)
                else:
                    near(2, bit >> 8, bit, span)

    for half in range(2):
        part = pl.ds(16 * half, 16)
        keys_out[half] = keys[part].reshape(LANES, LANES).T
        values_out[half] = values[part].reshape(LANES, LANES).T


def sort_probes(first, planes, full, rows, cols, probes):
    shape = (BLOCKS, 8, LANES)
    assert probes[0].size == 1 << SORT_BITS
    vmem = pl.BlockSpec(memory_space=pltpu.VMEM)
    sizes = (2, LANES, LANES)
    return pl.pallas_call(
        functools.partial(
            sort_kernel, planes, full, log2_of(cols), log2_of(rows) + log2_of(cols)
        ),
        out_shape=(
            jax.ShapeDtypeStruct(sizes, jnp.int32),
            jax.ShapeDtypeStruct(sizes, jnp.float32),
        ),
        in_specs=[pl.BlockSpec(memory_space=pltpu.SMEM)] + [vmem] * 5,
        out_specs=(vmem, vmem),
        scratch_shapes=[pltpu.VMEM(shape, jnp.int32), pltpu.VMEM(shape, jnp.float32)],
        compiler_params=pltpu.CompilerParams(vmem_limit_bytes=VMEM_LIMIT),
        cost_estimate=pl.CostEstimate(
            flops=2000 << SORT_BITS, bytes_accessed=28 << SORT_BITS, transcendentals=0
        ),
        name="sort_probes",
    )(first, *[array.reshape(shape) for array in probes])


def bins_kernel(planes, row_bits, col_bits, starts, keys, values, counts, sums):
    rows, cols = 1 << row_bits, 1 << col_bits
    blocks = 2 * LANES
    span = 2 * LANES
    number = pl.program_id(0)
    bucket = jnp.where(number < planes - 4, planes + 2 + number, number - (planes - 4) + 3)
    first, last = starts[bucket], starts[bucket + 1]
    block = first // LANES
    lane_rows = lax.broadcasted_iota(jnp.int32, (rows, span), 0)
    lane_cols = lax.broadcasted_iota(jnp.int32, (cols, span), 0)

    def chunk(ref, index):
        return ref[index & 1, pl.ds(jnp.right_shift(index, 1), 1), :]

    def partial(index):
        at = [jnp.minimum(index + i, blocks - 1) for i in range(2)]
        own = [
            jnp.right_shift(chunk(keys, at[i]), col_bits + row_bits)
            == jnp.where(index + i < blocks, bucket, -1)
            for i in range(2)
        ]
        key = [chunk(keys, i) for i in at]
        row = jnp.concatenate(
            [
                jnp.where(mine, jnp.right_shift(k, col_bits) & (rows - 1), -1)
                for mine, k in zip(own, key)
            ],
            axis=1,
        )
        col = jnp.concatenate(key, axis=1) & (cols - 1)
        value = jnp.concatenate([chunk(values, i) for i in at], axis=1)
        high = value.astype(jnp.bfloat16).astype(jnp.float32)
        rest = value - high
        row_hot = jnp.where(lane_rows == row, 1.0, 0.0).astype(jnp.bfloat16)
        col_hit = lane_cols == col

        def hot(v):
            return jnp.where(col_hit, v, 0.0).astype(jnp.bfloat16)

        def product(a, b):
            return lax.dot_general(
                a, b, (((1,), (1,)), ((), ())), preferred_element_type=jnp.float32
            )

        return product(row_hot, hot(1.0)), product(
            jnp.concatenate([row_hot, row_hot], axis=1),
            jnp.concatenate([hot(high), hot(rest)], axis=1),
        )

    counts[0], sums[0] = partial(block)

    @pl.loop(1, jnp.maximum((last + span - 1 - block * LANES) // span, 1))
    def _(turn):
        count, total = partial(block + 2 * turn)
        counts[0] += count
        sums[0] += total


def bins(starts, keys, values, planes, rows, cols):
    total = 2 * planes - 10
    vmem = pl.BlockSpec(memory_space=pltpu.VMEM)
    return pl.pallas_call(
        functools.partial(bins_kernel, planes, log2_of(rows), log2_of(cols)),
        grid=(total,),
        out_shape=(jax.ShapeDtypeStruct((total, rows, cols), jnp.float32),) * 2,
        in_specs=[pl.BlockSpec(memory_space=pltpu.SMEM), vmem, vmem],
        out_specs=(pl.BlockSpec((1, rows, cols), lambda i: (i, 0, 0)),) * 2,
        compiler_params=pltpu.CompilerParams(vmem_limit_bytes=VMEM_LIMIT),
        cost_estimate=pl.CostEstimate(
            flops=total * rows * cols * 1536, bytes_accessed=total * rows * cols * 8, transcendentals=0
        ),
        name="bins",
    )(starts, keys, values)


def field_kernel(
    place,
    velocity,
    profile,
    rate_ref,
    init_ref,
    below,
    above,
    count_fields,
    sum_fields,
    out,
    kappa,
    state0,
    state1,
    adjoint2,
    adjoint1,
    face_z,
    face_x,
    face_y,
    wind,
    sums,
    injects,
    sems,
    probe_sems,
):
    slab, rows, cols = rate_ref.shape
    planes = slab + 2 * HALO

    def fetch(number):
        slot = lax.rem(number, AHEAD)
        return [
            pltpu.make_async_copy(
                source.at[number], injects.at[slot, i], probe_sems.at[slot, i]
            )
            for i, source in enumerate((count_fields, sum_fields))
        ]

    copies = []
    for number, (own, target) in enumerate(((rate_ref, kappa), (init_ref, state0))):
        for part, (source, first, count) in enumerate(
            (
                (own, HALO, slab),
                (below.at[number], 0, HALO),
                (above.at[number], HALO + slab, HALO),
            )
        ):
            copy = pltpu.make_async_copy(
                source, target.at[pl.ds(first, count)], sems.at[3 * number + part]
            )
            copy.start()
            copies.append(copy)
    for number in range(AHEAD):
        for copy in fetch(number):
            copy.start()
    for copy in copies[:3]:
        copy.wait()

    starting = range(0, rows, STRIP)
    half = 0.5 * TIME_STEP

    def window(ref, z, r, after=True):
        pieces = [ref[z, pl.ds((r - 8) % rows, 8), :], ref[z, pl.ds(r, STRIP), :]]
        if after:
            pieces.append(ref[z, pl.ds((r + STRIP) % rows, 8), :])
        return jnp.concatenate(pieces, axis=0)

    def steps_down(wide):
        return (pltpu.roll(wide, wide.shape[0] - 1, 0) - wide)[: STRIP + 8]

    def with_previous(flux):
        return flux[8:], pltpu.roll(flux, 1, 0)[8:]

    def ahead(v):
        return pltpu.roll(v, cols - 1, 1)

    def behind(v):
        return pltpu.roll(v, 1, 1)

    @pl.loop(0, planes)
    def _(z):
        for r in starting:
            part = pl.ds(r, STRIP)
            kappa[z, part, :] = jnp.exp(kappa[z, part, :])

    @pl.loop(0, planes - 1)
    def _(z):
        for r in starting:
            part = pl.ds(r, STRIP)
            wide = window(kappa, z, r)
            k = wide[8 : 8 + STRIP]
            face_z[z, part, :] = half * (k + kappa[z + 1, part, :])
            face_x[z, part, :] = half * (k + pltpu.roll(wide, STRIP + 15, 0)[8 : 8 + STRIP])
            face_y[z, part, :] = half * (k + ahead(k))

    for copy in copies[3:]:
        copy.wait()

    for r in starting:
        part = pl.ds(r, STRIP)
        wind[part, :] = TIME_STEP * velocity[part, :]

    def stepped(ref, z, r, forward):
        part = pl.ds(r, STRIP)
        wide = window(ref, z, r)
        v = wide[8 : 8 + STRIP]
        upper, lower = face_z[z, part, :], face_z[z - 1, part, :]
        if forward:
            lower = lower + wind[part, :]
        else:
            upper = upper + wind[part, :]
        total = upper * (ref[z + 1, part, :] - v) - lower * (v - ref[z - 1, part, :])
        flux, previous = with_previous(window(face_x, z, r, False) * steps_down(wide))
        total = total + (flux - previous)
        flux = face_y[z, part, :] * (ahead(v) - v)
        return v + (total + (flux - behind(flux)))

    source_plane = place[0]

    def forward(ref, z, r):
        scale = jnp.where(z == source_plane, jnp.float32(TIME_STEP), jnp.float32(0.0))
        return stepped(ref, z, r, True) + scale * profile[pl.ds(r, STRIP), :]

    @pl.loop(1, planes - 1)
    def _(z):
        for r in starting:
            state1[z, pl.ds(r, STRIP), :] = forward(state0, z, r)

    def probes(number):
        for copy in fetch(number):
            copy.wait()
        return lax.rem(number, AHEAD)

    def refill(number):
        @pl.when(number + AHEAD < count_fields.shape[0])
        def _():
            for copy in fetch(number + AHEAD):
                copy.start()

    @pl.loop(2, planes - 2)
    def _(z):
        number = z - 2
        slot = probes(number)
        for r in starting:
            part = pl.ds(r, STRIP)
            count, total = injects[slot, 0, part, :], injects[slot, 1, part, :]
            adjoint2[z, part, :] = count * forward(state1, z, r) - total
        refill(number)

    @pl.loop(3, planes - 3)
    def _(z):
        number = planes - 4 + z - 3
        slot = probes(number)
        for r in starting:
            part = pl.ds(r, STRIP)
            inject = injects[slot, 0, part, :] * state1[z, part, :] - injects[slot, 1, part, :]
            adjoint1[z, part, :] = stepped(adjoint2, z, r, False) + inject
        refill(number)

    fields = ((state1, adjoint2), (state0, adjoint1))

    def upward(z, part):
        return sum(
            (state[z + 1, part, :] - state[z, part, :])
            * (adjoint[z + 1, part, :] - adjoint[z, part, :])
            for state, adjoint in fields
        )

    def level(z, r):
        wide = [(window(state, z, r), window(adjoint, z, r)) for state, adjoint in fields]
        flux, previous = with_previous(sum(steps_down(c) * steps_down(m) for c, m in wide))
        total = flux + previous
        inner = [(c[8 : 8 + STRIP], m[8 : 8 + STRIP]) for c, m in wide]
        flux = sum((ahead(c) - c) * (ahead(m) - m) for c, m in inner)
        return total + (flux + behind(flux))

    def pool(length):
        shape = (length, length // R)
        fine = lax.broadcasted_iota(jnp.int32, shape, 0)
        coarse = lax.broadcasted_iota(jnp.int32, shape, 1)
        return jnp.where((fine >= coarse * R) & (fine < coarse * R + R), 1.0, 0.0)

    def exact(a, b, dims):
        return lax.dot_general(
            a,
            b,
            (dims, ((), ())),
            precision=lax.Precision.HIGHEST,
            preferred_element_type=jnp.float32,
        )

    @pl.loop(0, slab // R)
    def _(number):
        for r in starting:
            part = pl.ds(r, STRIP)
            both = jnp.zeros((STRIP, cols), jnp.float32)
            below = upward(HALO + number * R - 1, part)
            for layer in range(R):
                z = HALO + number * R + layer
                above = upward(z, part)
                both = both + kappa[z, part, :] * (level(z, r) + (below + above))
                below = above
            sums[part, :] = (-half) * both
        narrow = exact(sums[...], pool(cols), ((1,), (0,)))
        out[number] = exact(pool(rows), narrow, ((0,), (0,)))


def fields(place, velocity, profile, rate, init, below, above, counts, sums):
    slab, rows, cols = rate.shape
    planes = slab + 2 * HALO
    smem = pl.BlockSpec(memory_space=pltpu.SMEM)
    vmem = pl.BlockSpec(memory_space=pltpu.VMEM)
    anywhere = pl.BlockSpec(memory_space=pl.ANY)
    field = pltpu.VMEM((planes, rows, cols), jnp.float32)
    plane = pltpu.VMEM((rows, cols), jnp.float32)
    return pl.pallas_call(
        field_kernel,
        out_shape=jax.ShapeDtypeStruct((slab // R, rows // R, cols // R), jnp.float32),
        in_specs=[smem] + [vmem] * 2 + [anywhere] * 6,
        out_specs=vmem,
        scratch_shapes=[field] * 8
        + [plane] * 2
        + [
            pltpu.VMEM((AHEAD, 2, rows, cols), jnp.float32),
            pltpu.SemaphoreType.DMA((6,)),
            pltpu.SemaphoreType.DMA((AHEAD, 2)),
        ],
        compiler_params=pltpu.CompilerParams(vmem_limit_bytes=VMEM_LIMIT),
        cost_estimate=pl.CostEstimate(
            flops=planes * rows * cols * 200,
            bytes_accessed=planes * rows * cols * 8,
            transcendentals=planes * rows * cols,
        ),
        name="fields",
    )(place, velocity, profile, rate, init, below, above, counts, sums)


def tail_kernel(
    domains,
    tracers,
    coarse,
    weights,
    x_table,
    y_table,
    z_table,
    out,
    send_sum,
    recv_sum,
    send_z,
    recv_z,
    send_back,
    recv_back,
    send_x,
    recv_x,
    sum_sems,
    z_sems,
    back_sems,
    x_sems,
):
    depth, x_size, y_size = coarse.shape
    y_share, x_share = y_size // tracers, x_size // tracers
    y_own = y_share // domains
    z_size = depth * domains
    tracer, domain = lax.axis_index("tracer"), lax.axis_index("domain")

    barrier = pltpu.get_barrier_semaphore()
    for axis, me, count in (("tracer", tracer, tracers), ("domain", domain, domains)):
        for i in range(1, count):
            pl.semaphore_signal(
                barrier,
                inc=1,
                device_id={axis: lax.rem(me + i, count)},
                device_id_type=pl.DeviceIdType.MESH,
            )
    pl.semaphore_wait(barrier, tracers + domains - 2)

    def exact(a, b, dims):
        return lax.dot_general(
            a,
            b,
            (dims, ((), ())),
            precision=lax.Precision.HIGHEST,
            preferred_element_type=jnp.float32,
        )

    def exchange(axis, me, count, source, target, sems):
        copies = []
        for i in range(1, count):
            peer = lax.rem(me + i, count)
            copy = pltpu.make_async_remote_copy(
                src_ref=source(peer),
                dst_ref=target(i, me),
                send_sem=sems.at[0, i],
                recv_sem=sems.at[1, i],
                device_id={axis: peer},
                device_id_type=pl.DeviceIdType.MESH,
            )
            copy.start()
            copies.append(copy)
        return copies

    spectral = exact(y_table[...], coarse[...].reshape(depth * x_size, y_size), ((1,), (1,)))
    for block in range(tracers):
        send_sum[block] = spectral[block * y_share : (block + 1) * y_share]
    first = exchange(
        "tracer",
        tracer,
        tracers,
        lambda peer: send_sum.at[peer],
        lambda i, me: recv_sum.at[i],
        sum_sems,
    )
    total = send_sum[tracer]
    for i, copy in enumerate(first):
        copy.wait_recv()
        total = total + recv_sum[i + 1]

    for z in range(depth):
        send_z[:, z, :] = exact(
            total[:, z * x_size : (z + 1) * x_size], x_table[...], ((1,), (0,))
        )
    second = exchange(
        "domain",
        domain,
        domains,
        lambda peer: send_z.at[pl.ds(peer * y_own, y_own)],
        lambda i, me: recv_z.at[me],
        z_sems,
    )
    recv_z[domain] = send_z[pl.ds(domain * y_own, y_own)]
    for copy in second:
        copy.wait_recv()

    for k in range(y_own):
        column = recv_z[:, k].reshape(z_size, x_size)
        column = exact(z_table[...], column, ((1,), (0,))) * weights[k]
        column = exact(z_table[...], column, ((1,), (0,)))
        send_back[:, k] = column.reshape(domains, depth, x_size)
    third = exchange(
        "domain",
        domain,
        domains,
        lambda peer: send_back.at[peer],
        lambda i, me: recv_back.at[pl.ds(me * y_own, y_own)],
        back_sems,
    )
    recv_back[pl.ds(domain * y_own, y_own)] = send_back[domain]
    for copy in third:
        copy.wait_recv()

    spectral = jnp.concatenate([recv_back[:, z, :] for z in range(depth)], axis=0)
    spectral = exact(x_table[...], spectral, ((1,), (1,)))
    for block in range(tracers):
        send_x[block] = spectral[block * x_share : (block + 1) * x_share]
    fourth = exchange(
        "tracer",
        tracer,
        tracers,
        lambda peer: send_x.at[peer],
        lambda i, me: recv_x.at[me],
        x_sems,
    )
    recv_x[tracer] = send_x[tracer]
    for copy in fourth:
        copy.wait_recv()

    for z in range(depth):
        lanes = slice(z * y_share, (z + 1) * y_share)
        row = jnp.concatenate([recv_x[i][:, lanes] for i in range(tracers)], axis=1)
        out[z] = exact(row, y_table[...], ((1,), (0,)))
    for copy in first + second + third + fourth:
        copy.wait_send()


def filtered(coarse, weights, x_table, y_table, z_table):
    depth, x_size, y_size = coarse.shape
    domains, tracers = lax.axis_size("domain"), lax.axis_size("tracer")
    y_share, x_share = y_size // tracers, x_size // tracers
    y_own = y_share // domains
    vmem = pl.BlockSpec(memory_space=pltpu.VMEM)

    def buffer(*shape):
        return pltpu.VMEM(shape, jnp.float32)

    def sems(count):
        return pltpu.SemaphoreType.DMA((2, count))

    return pl.pallas_call(
        functools.partial(tail_kernel, domains, tracers),
        out_shape=jax.ShapeDtypeStruct((depth, x_share, y_size), jnp.float32),
        in_specs=[vmem] * 5,
        out_specs=vmem,
        scratch_shapes=[
            buffer(tracers, y_share, depth * x_size),
            buffer(tracers, y_share, depth * x_size),
            buffer(y_share, depth, x_size),
            buffer(domains, y_own, depth, x_size),
            buffer(domains, y_own, depth, x_size),
            buffer(y_share, depth, x_size),
            buffer(tracers, x_share, depth * y_share),
            buffer(tracers, x_share, depth * y_share),
            sems(tracers),
            sems(domains),
            sems(domains),
            sems(tracers),
        ],
        compiler_params=pltpu.CompilerParams(
            collective_id=1, has_side_effects=True, vmem_limit_bytes=VMEM_LIMIT
        ),
        cost_estimate=pl.CostEstimate(
            flops=coarse.size * 3000, bytes_accessed=coarse.size * 8, transcendentals=0
        ),
        name="filtered",
    )(coarse, weights, x_table, y_table, z_table)


def halos(arrays, axis, width):
    count, length = lax.axis_size(axis), arrays[0].shape[0]
    up = [(i, (i + 1) % count) for i in range(count)]
    down = [(j, i) for i, j in up]
    last = jnp.stack([array[length - width :] for array in arrays])
    initial = jnp.stack([array[:width] for array in arrays])
    return lax.ppermute(last, axis, up), lax.ppermute(initial, axis, down)


def hartley(length, first_row, count):
    indices = first_row + lax.iota(jnp.int32, count)
    phases = indices[:, None] * lax.iota(jnp.int32, length)[None, :] % length
    angles = 2.0 * math.pi / length * phases.astype(jnp.float32)
    return jnp.cos(angles) + jnp.sin(angles)


def symbol_part(length, first_row, count):
    indices = (first_row + lax.iota(jnp.int32, count)) % length
    angles = 2.0 * math.pi / length * indices.astype(jnp.float32)
    return 2.0 - 2.0 * jnp.cos(angles)


def local(log_rate, velocity, initial, profile, plane, depth, row, column, step_of, observed):
    slab, rows, cols = log_rate.shape
    domains, tracers = lax.axis_size("domain"), lax.axis_size("tracer")
    full = slab * domains
    planes = slab + 2 * HALO
    first = lax.axis_index("domain") * slab - HALO
    below, above = halos((log_rate, initial[0]), "domain", HALO)

    keys, values = sort_probes(
        first.reshape(1), planes, full, rows, cols, (depth, row, column, step_of, observed)
    )
    edges = lax.iota(jnp.int32, STEPS * planes + 1) * (rows * cols)
    starts = jnp.sum((keys[None] < edges[:, None, None, None]).astype(jnp.int32), axis=(1, 2, 3))
    place = (plane - first + full) % full

    counts, sums = bins(starts, keys, values, planes, rows, cols)
    coarse = fields(place, velocity, profile[0], log_rate, initial[0], below, above, counts, sums)

    x_size, y_size, z_size = rows // R, cols // R, full // R
    y_own = y_size // (tracers * domains)
    own_first = (lax.axis_index("tracer") * domains + lax.axis_index("domain")) * y_own
    lam = (
        symbol_part(y_size, own_first, y_own)[:, None, None]
        + symbol_part(z_size, 0, z_size)[None, :, None]
        + symbol_part(x_size, 0, x_size)[None, None, :]
    )
    factor = 1.0 + PRIOR_RANGE * lam
    weights = 1.0 / (factor * factor) / (x_size * y_size * z_size)
    tables = [hartley(size, 0, size) for size in (x_size, y_size, z_size)]
    return filtered(coarse, weights, *tables)


def solution(mesh):
    return jax.shard_map(
        local,
        mesh=mesh,
        in_specs=(
            P("domain", None, None),
            P(),
            P("tracer", "domain", None, None),
            P("tracer", None, None),
            P("tracer"),
            P("tracer", None),
            P("tracer", None),
            P("tracer", None),
            P("tracer", None),
            P("tracer", None),
        ),
        out_specs=P("domain", "tracer", None),
        check_vma=False,
    )
```

```python
import functools
import math

import jax
import jax.numpy as jnp
from jax import lax
from jax.experimental import pallas as pl
from jax.experimental.pallas import tpu as pltpu
from jax.sharding import PartitionSpec as P

R = 2
STEPS = 2
HALO = 2 * STEPS
STRIP = 32
LANES = 128
AHEAD = 4
SORT_BITS = 15
BLOCKS = (1 << SORT_BITS) // (8 * LANES)
VMEM_LIMIT = 60 * 1024 * 1024

TIME_STEP = 0.14
PRIOR_RANGE = 4.0


def log2_of(size):
    bits = size.bit_length() - 1
    assert size == 1 << bits
    return bits


def sort_kernel(
    planes,
    full,
    shift_row,
    shift_bucket,
    first,
    depth,
    row,
    column,
    step,
    observed,
    keys_out,
    values_out,
    keys,
    values,
):
    layer = depth[...] - first[0]
    layer = jnp.where(layer < 0, layer + full, layer)
    layer = jnp.where(layer >= full, layer - full, layer)
    bucket = jnp.where(layer < planes, (step[...] - 1) * planes + layer, STEPS * planes)
    keys[...] = (
        jnp.left_shift(bucket, shift_bucket) | jnp.left_shift(row[...], shift_row) | column[...]
    )
    values[...] = observed[...]
    group = 8

    def index_of(start, count):
        shape = (count, 8, LANES)
        major = start + lax.broadcasted_iota(jnp.int32, shape, 0)
        return (
            (major & 15)
            | jnp.left_shift(lax.broadcasted_iota(jnp.int32, shape, 1), 4)
            | jnp.left_shift(jnp.right_shift(major, 4), 7)
            | jnp.left_shift(lax.broadcasted_iota(jnp.int32, shape, 2), 8)
        )

    def far(distance, span):
        for begin in range(0, BLOCKS, 2 * distance):
            for start in range(begin, begin + distance, group):
                count = min(group, distance)
                low, high = pl.ds(start, count), pl.ds(start + distance, count)
                a, b, x, y = keys[low], keys[high], values[low], values[high]
                up = (index_of(start, count) & span) == 0
                swap = (up & (a > b)) | (jnp.logical_not(up) & (b > a))
                keys[low] = jnp.where(swap, b, a)
                keys[high] = jnp.where(swap, a, b)
                values[low] = jnp.where(swap, y, x)
                values[high] = jnp.where(swap, x, y)

    def near(axis, shift, bit, span):
        size = 8 if axis == 1 else LANES
        for start in range(0, BLOCKS, group):
            part = pl.ds(start, group)
            a, x = keys[part], values[part]
            index = index_of(start, group)
            upper = (index & bit) != 0
            keep_min = ((index & span) == 0) != upper

            def partner(v):
                return jnp.where(
                    upper, pltpu.roll(v, shift, axis), pltpu.roll(v, size - shift, axis)
                )

            b, y = partner(a), partner(x)
            swap = (keep_min & (b < a)) | (jnp.logical_not(keep_min) & (b > a))
            keys[part] = jnp.where(swap, b, a)
            values[part] = jnp.where(swap, y, x)

    @pl.loop(0, SORT_BITS)
    def _(phase):
        span = jnp.left_shift(jnp.int32(1), phase + 1)
        for q in reversed(range(SORT_BITS)):

            @pl.when(q <= phase)
            def _():
                bit = 1 << q
                if q < 4:
                    far(bit, span)
                elif q == 7:
                    far(16, span)
                elif q < 7:
                    near(1, bit >> 4, bit, span)
                else:
                    near(2, bit >> 8, bit, span)

    for half in range(2):
        part = pl.ds(16 * half, 16)
        keys_out[half] = keys[part].reshape(LANES, LANES).T
        values_out[half] = values[part].reshape(LANES, LANES).T


def sort_probes(first, planes, full, rows, cols, probes):
    shape = (BLOCKS, 8, LANES)
    assert probes[0].size == 1 << SORT_BITS
    vmem = pl.BlockSpec(memory_space=pltpu.VMEM)
    sizes = (2, LANES, LANES)
    return pl.pallas_call(
        functools.partial(
            sort_kernel, planes, full, log2_of(cols), log2_of(rows) + log2_of(cols)
        ),
        out_shape=(
            jax.ShapeDtypeStruct(sizes, jnp.int32),
            jax.ShapeDtypeStruct(sizes, jnp.float32),
        ),
        in_specs=[pl.BlockSpec(memory_space=pltpu.SMEM)] + [vmem] * 5,
        out_specs=(vmem, vmem),
        scratch_shapes=[pltpu.VMEM(shape, jnp.int32), pltpu.VMEM(shape, jnp.float32)],
        compiler_params=pltpu.CompilerParams(vmem_limit_bytes=VMEM_LIMIT),
        cost_estimate=pl.CostEstimate(
            flops=2000 << SORT_BITS, bytes_accessed=28 << SORT_BITS, transcendentals=0
        ),
        name="sort_probes",
    )(first, *[array.reshape(shape) for array in probes])


def bins_kernel(planes, row_bits, col_bits, starts, keys, values, counts, sums):
    rows, cols = 1 << row_bits, 1 << col_bits
    blocks = 2 * LANES
    span = 2 * LANES
    number = pl.program_id(0)
    bucket = jnp.where(number < planes - 4, planes + 2 + number, number - (planes - 4) + 3)
    first, last = starts[bucket], starts[bucket + 1]
    block = first // LANES
    lane_rows = lax.broadcasted_iota(jnp.int32, (rows, span), 0)
    lane_cols = lax.broadcasted_iota(jnp.int32, (cols, span), 0)

    def chunk(ref, index):
        return ref[index & 1, pl.ds(jnp.right_shift(index, 1), 1), :]

    def partial(index):
        at = [jnp.minimum(index + i, blocks - 1) for i in range(2)]
        own = [
            jnp.right_shift(chunk(keys, at[i]), col_bits + row_bits)
            == jnp.where(index + i < blocks, bucket, -1)
            for i in range(2)
        ]
        key = [chunk(keys, i) for i in at]
        row = jnp.concatenate(
            [
                jnp.where(mine, jnp.right_shift(k, col_bits) & (rows - 1), -1)
                for mine, k in zip(own, key)
            ],
            axis=1,
        )
        col = jnp.concatenate(key, axis=1) & (cols - 1)
        value = jnp.concatenate([chunk(values, i) for i in at], axis=1)
        high = value.astype(jnp.bfloat16).astype(jnp.float32)
        rest = value - high
        row_hot = jnp.where(lane_rows == row, 1.0, 0.0).astype(jnp.bfloat16)
        col_hit = lane_cols == col

        def hot(v):
            return jnp.where(col_hit, v, 0.0).astype(jnp.bfloat16)

        def product(a, b):
            return lax.dot_general(
                a, b, (((1,), (1,)), ((), ())), preferred_element_type=jnp.float32
            )

        return product(row_hot, hot(1.0)), product(
            jnp.concatenate([row_hot, row_hot], axis=1),
            jnp.concatenate([hot(high), hot(rest)], axis=1),
        )

    counts[0], sums[0] = partial(block)

    @pl.loop(1, jnp.maximum((last + span - 1 - block * LANES) // span, 1))
    def _(turn):
        count, total = partial(block + 2 * turn)
        counts[0] += count
        sums[0] += total


def bins(starts, keys, values, planes, rows, cols):
    total = 2 * planes - 10
    vmem = pl.BlockSpec(memory_space=pltpu.VMEM)
    return pl.pallas_call(
        functools.partial(bins_kernel, planes, log2_of(rows), log2_of(cols)),
        grid=(total,),
        out_shape=(jax.ShapeDtypeStruct((total, rows, cols), jnp.float32),) * 2,
        in_specs=[pl.BlockSpec(memory_space=pltpu.SMEM), vmem, vmem],
        out_specs=(pl.BlockSpec((1, rows, cols), lambda i: (i, 0, 0)),) * 2,
        compiler_params=pltpu.CompilerParams(vmem_limit_bytes=VMEM_LIMIT),
        cost_estimate=pl.CostEstimate(
            flops=total * rows * cols * 1536, bytes_accessed=total * rows * cols * 8, transcendentals=0
        ),
        name="bins",
    )(starts, keys, values)


def field_kernel(
    place,
    velocity,
    profile,
    rate_ref,
    init_ref,
    below,
    above,
    count_fields,
    sum_fields,
    out,
    kappa,
    state0,
    state1,
    adjoint2,
    adjoint1,
    face_z,
    face_x,
    face_y,
    wind,
    sums,
    narrow,
    injects,
    sems,
    probe_sems,
):
    slab, rows, cols = rate_ref.shape
    planes = slab + 2 * HALO

    def fetch(number):
        slot = lax.rem(number, AHEAD)
        return [
            pltpu.make_async_copy(
                source.at[number], injects.at[slot, i], probe_sems.at[slot, i]
            )
            for i, source in enumerate((count_fields, sum_fields))
        ]

    copies = []
    for number, (own, target) in enumerate(((rate_ref, kappa), (init_ref, state0))):
        for part, (source, first, count) in enumerate(
            (
                (own, HALO, slab),
                (below.at[number], 0, HALO),
                (above.at[number], HALO + slab, HALO),
            )
        ):
            copy = pltpu.make_async_copy(
                source, target.at[pl.ds(first, count)], sems.at[3 * number + part]
            )
            copy.start()
            copies.append(copy)
    for number in range(AHEAD):
        for copy in fetch(number):
            copy.start()
    for copy in copies[:3]:
        copy.wait()

    starting = range(0, rows, STRIP)
    half = 0.5 * TIME_STEP

    def window(ref, z, r, after=True):
        pieces = [ref[z, pl.ds((r - 8) % rows, 8), :], ref[z, pl.ds(r, STRIP), :]]
        if after:
            pieces.append(ref[z, pl.ds((r + STRIP) % rows, 8), :])
        return jnp.concatenate(pieces, axis=0)

    def steps_down(wide):
        return (pltpu.roll(wide, wide.shape[0] - 1, 0) - wide)[: STRIP + 8]

    def with_previous(flux):
        return flux[8:], pltpu.roll(flux, 1, 0)[8:]

    def ahead(v):
        return pltpu.roll(v, cols - 1, 1)

    def behind(v):
        return pltpu.roll(v, 1, 1)

    @pl.loop(0, planes)
    def _(z):
        for r in starting:
            part = pl.ds(r, STRIP)
            kappa[z, part, :] = jnp.exp(kappa[z, part, :])

    @pl.loop(0, planes - 1)
    def _(z):
        for r in starting:
            part = pl.ds(r, STRIP)
            wide = window(kappa, z, r)
            k = wide[8 : 8 + STRIP]
            face_z[z, part, :] = half * (k + kappa[z + 1, part, :])
            face_x[z, part, :] = half * (k + pltpu.roll(wide, STRIP + 15, 0)[8 : 8 + STRIP])
            face_y[z, part, :] = half * (k + ahead(k))

    for copy in copies[3:]:
        copy.wait()

    for r in starting:
        part = pl.ds(r, STRIP)
        wind[part, :] = TIME_STEP * velocity[part, :]

    def stepped(ref, z, r, forward):
        part = pl.ds(r, STRIP)
        wide = window(ref, z, r)
        v = wide[8 : 8 + STRIP]
        upper, lower = face_z[z, part, :], face_z[z - 1, part, :]
        if forward:
            lower = lower + wind[part, :]
        else:
            upper = upper + wind[part, :]
        total = upper * (ref[z + 1, part, :] - v) - lower * (v - ref[z - 1, part, :])
        flux, previous = with_previous(window(face_x, z, r, False) * steps_down(wide))
        total = total + (flux - previous)
        flux = face_y[z, part, :] * (ahead(v) - v)
        return v + (total + (flux - behind(flux)))

    source_plane = place[0]

    def forward(ref, z, r):
        scale = jnp.where(z == source_plane, jnp.float32(TIME_STEP), jnp.float32(0.0))
        return stepped(ref, z, r, True) + scale * profile[pl.ds(r, STRIP), :]

    @pl.loop(1, planes - 1)
    def _(z):
        for r in starting:
            state1[z, pl.ds(r, STRIP), :] = forward(state0, z, r)

    def probes(number):
        for copy in fetch(number):
            copy.wait()
        return lax.rem(number, AHEAD)

    def refill(number):
        @pl.when(number + AHEAD < count_fields.shape[0])
        def _():
            for copy in fetch(number + AHEAD):
                copy.start()

    @pl.loop(2, planes - 2)
    def _(z):
        number = z - 2
        slot = probes(number)
        for r in starting:
            part = pl.ds(r, STRIP)
            count, total = injects[slot, 0, part, :], injects[slot, 1, part, :]
            adjoint2[z, part, :] = count * forward(state1, z, r) - total
        refill(number)

    @pl.loop(3, planes - 3)
    def _(z):
        number = planes - 4 + z - 3
        slot = probes(number)
        for r in starting:
            part = pl.ds(r, STRIP)
            inject = injects[slot, 0, part, :] * state1[z, part, :] - injects[slot, 1, part, :]
            adjoint1[z, part, :] = stepped(adjoint2, z, r, False) + inject
        refill(number)

    fields = ((state1, adjoint2), (state0, adjoint1))

    def upward(z, part):
        return sum(
            (state[z + 1, part, :] - state[z, part, :])
            * (adjoint[z + 1, part, :] - adjoint[z, part, :])
            for state, adjoint in fields
        )

    def level(z, r):
        wide = [(window(state, z, r), window(adjoint, z, r)) for state, adjoint in fields]
        flux, previous = with_previous(sum(steps_down(c) * steps_down(m) for c, m in wide))
        total = flux + previous
        inner = [(c[8 : 8 + STRIP], m[8 : 8 + STRIP]) for c, m in wide]
        flux = sum((ahead(c) - c) * (ahead(m) - m) for c, m in inner)
        return total + (flux + behind(flux))

    def pool(length):
        shape = (length, length // R)
        fine = lax.broadcasted_iota(jnp.int32, shape, 0)
        coarse = lax.broadcasted_iota(jnp.int32, shape, 1)
        return jnp.where((fine >= coarse * R) & (fine < coarse * R + R), 1.0, 0.0)

    pairs = jnp.concatenate([pool(cols).astype(jnp.bfloat16)] * 3, axis=0)

    @pl.loop(0, slab // R)
    def _(number):
        for r in starting:
            part = pl.ds(r, STRIP)
            both = jnp.zeros((STRIP, cols), jnp.float32)
            below = upward(HALO + number * R - 1, part)
            for layer in range(R):
                z = HALO + number * R + layer
                above = upward(z, part)
                both = both + kappa[z, part, :] * (level(z, r) + (below + above))
                below = above
            sums[part, :] = (-half) * both
        whole = sums[...]
        high = whole.astype(jnp.bfloat16)
        rest = whole - high.astype(jnp.float32)
        middle = rest.astype(jnp.bfloat16)
        low = (rest - middle.astype(jnp.float32)).astype(jnp.bfloat16)
        narrow[...] = jnp.dot(
            jnp.concatenate([high, middle, low], axis=1),
            pairs,
            preferred_element_type=jnp.float32,
        )
        out[number] = sum(narrow[pl.ds(i, rows // R, stride=R), :] for i in range(R))


def fields(place, velocity, profile, rate, init, below, above, counts, sums):
    slab, rows, cols = rate.shape
    planes = slab + 2 * HALO
    smem = pl.BlockSpec(memory_space=pltpu.SMEM)
    vmem = pl.BlockSpec(memory_space=pltpu.VMEM)
    anywhere = pl.BlockSpec(memory_space=pl.ANY)
    field = pltpu.VMEM((planes, rows, cols), jnp.float32)
    plane = pltpu.VMEM((rows, cols), jnp.float32)
    return pl.pallas_call(
        field_kernel,
        out_shape=jax.ShapeDtypeStruct((slab // R, rows // R, cols // R), jnp.float32),
        in_specs=[smem] + [vmem] * 2 + [anywhere] * 6,
        out_specs=vmem,
        scratch_shapes=[field] * 8
        + [plane] * 2
        + [
            pltpu.VMEM((rows, cols // R), jnp.float32),
            pltpu.VMEM((AHEAD, 2, rows, cols), jnp.float32),
            pltpu.SemaphoreType.DMA((6,)),
            pltpu.SemaphoreType.DMA((AHEAD, 2)),
        ],
        compiler_params=pltpu.CompilerParams(vmem_limit_bytes=VMEM_LIMIT),
        cost_estimate=pl.CostEstimate(
            flops=planes * rows * cols * 200,
            bytes_accessed=planes * rows * cols * 8,
            transcendentals=planes * rows * cols,
        ),
        name="fields",
    )(place, velocity, profile, rate, init, below, above, counts, sums)


def tail_kernel(
    domains,
    tracers,
    coarse,
    weights,
    x_table,
    y_table,
    z_table,
    out,
    send_sum,
    recv_sum,
    send_z,
    recv_z,
    send_back,
    recv_back,
    send_x,
    recv_x,
    sum_sems,
    z_sems,
    back_sems,
    x_sems,
):
    depth, x_size, y_size = coarse.shape
    y_share, x_share = y_size // tracers, x_size // tracers
    y_own = y_share // domains
    z_size = depth * domains
    tracer, domain = lax.axis_index("tracer"), lax.axis_index("domain")

    barrier = pltpu.get_barrier_semaphore()
    for axis, me, count in (("tracer", tracer, tracers), ("domain", domain, domains)):
        for i in range(1, count):
            pl.semaphore_signal(
                barrier,
                inc=1,
                device_id={axis: lax.rem(me + i, count)},
                device_id_type=pl.DeviceIdType.MESH,
            )
    pl.semaphore_wait(barrier, tracers + domains - 2)

    def exact(a, b, dims):
        return lax.dot_general(
            a,
            b,
            (dims, ((), ())),
            precision=lax.Precision.HIGHEST,
            preferred_element_type=jnp.float32,
        )

    def exchange(axis, me, count, source, target, sems):
        copies = []
        for i in range(1, count):
            peer = lax.rem(me + i, count)
            copy = pltpu.make_async_remote_copy(
                src_ref=source(peer),
                dst_ref=target(i, me),
                send_sem=sems.at[0, i],
                recv_sem=sems.at[1, i],
                device_id={axis: peer},
                device_id_type=pl.DeviceIdType.MESH,
            )
            copy.start()
            copies.append(copy)
        return copies

    spectral = exact(y_table[...], coarse[...].reshape(depth * x_size, y_size), ((1,), (1,)))
    for block in range(tracers):
        send_sum[block] = spectral[block * y_share : (block + 1) * y_share]
    first = exchange(
        "tracer",
        tracer,
        tracers,
        lambda peer: send_sum.at[peer],
        lambda i, me: recv_sum.at[i],
        sum_sems,
    )
    total = send_sum[tracer]
    for i, copy in enumerate(first):
        copy.wait_recv()
        total = total + recv_sum[i + 1]

    for z in range(depth):
        send_z[:, z, :] = exact(
            total[:, z * x_size : (z + 1) * x_size], x_table[...], ((1,), (0,))
        )
    second = exchange(
        "domain",
        domain,
        domains,
        lambda peer: send_z.at[pl.ds(peer * y_own, y_own)],
        lambda i, me: recv_z.at[me],
        z_sems,
    )
    recv_z[domain] = send_z[pl.ds(domain * y_own, y_own)]
    for copy in second:
        copy.wait_recv()

    for k in range(y_own):
        column = recv_z[:, k].reshape(z_size, x_size)
        column = exact(z_table[...], column, ((1,), (0,))) * weights[k]
        column = exact(z_table[...], column, ((1,), (0,)))
        send_back[:, k] = column.reshape(domains, depth, x_size)
    third = exchange(
        "domain",
        domain,
        domains,
        lambda peer: send_back.at[peer],
        lambda i, me: recv_back.at[pl.ds(me * y_own, y_own)],
        back_sems,
    )
    recv_back[pl.ds(domain * y_own, y_own)] = send_back[domain]
    for copy in third:
        copy.wait_recv()

    spectral = jnp.concatenate([recv_back[:, z, :] for z in range(depth)], axis=0)
    spectral = exact(x_table[...], spectral, ((1,), (1,)))
    for block in range(tracers):
        send_x[block] = spectral[block * x_share : (block + 1) * x_share]
    fourth = exchange(
        "tracer",
        tracer,
        tracers,
        lambda peer: send_x.at[peer],
        lambda i, me: recv_x.at[me],
        x_sems,
    )
    recv_x[tracer] = send_x[tracer]
    for copy in fourth:
        copy.wait_recv()

    for z in range(depth):
        lanes = slice(z * y_share, (z + 1) * y_share)
        row = jnp.concatenate([recv_x[i][:, lanes] for i in range(tracers)], axis=1)
        out[z] = exact(row, y_table[...], ((1,), (0,)))
    for copy in first + second + third + fourth:
        copy.wait_send()


def filtered(coarse, weights, x_table, y_table, z_table):
    depth, x_size, y_size = coarse.shape
    domains, tracers = lax.axis_size("domain"), lax.axis_size("tracer")
    y_share, x_share = y_size // tracers, x_size // tracers
    y_own = y_share // domains
    vmem = pl.BlockSpec(memory_space=pltpu.VMEM)

    def buffer(*shape):
        return pltpu.VMEM(shape, jnp.float32)

    def sems(count):
        return pltpu.SemaphoreType.DMA((2, count))

    return pl.pallas_call(
        functools.partial(tail_kernel, domains, tracers),
        out_shape=jax.ShapeDtypeStruct((depth, x_share, y_size), jnp.float32),
        in_specs=[vmem] * 5,
        out_specs=vmem,
        scratch_shapes=[
            buffer(tracers, y_share, depth * x_size),
            buffer(tracers, y_share, depth * x_size),
            buffer(y_share, depth, x_size),
            buffer(domains, y_own, depth, x_size),
            buffer(domains, y_own, depth, x_size),
            buffer(y_share, depth, x_size),
            buffer(tracers, x_share, depth * y_share),
            buffer(tracers, x_share, depth * y_share),
            sems(tracers),
            sems(domains),
            sems(domains),
            sems(tracers),
        ],
        compiler_params=pltpu.CompilerParams(
            collective_id=1, has_side_effects=True, vmem_limit_bytes=VMEM_LIMIT
        ),
        cost_estimate=pl.CostEstimate(
            flops=coarse.size * 3000, bytes_accessed=coarse.size * 8, transcendentals=0
        ),
        name="filtered",
    )(coarse, weights, x_table, y_table, z_table)


def halos(arrays, axis, width):
    count, length = lax.axis_size(axis), arrays[0].shape[0]
    up = [(i, (i + 1) % count) for i in range(count)]
    down = [(j, i) for i, j in up]
    last = jnp.stack([array[length - width :] for array in arrays])
    initial = jnp.stack([array[:width] for array in arrays])
    return lax.ppermute(last, axis, up), lax.ppermute(initial, axis, down)


def hartley(length, first_row, count):
    indices = first_row + lax.iota(jnp.int32, count)
    phases = indices[:, None] * lax.iota(jnp.int32, length)[None, :] % length
    angles = 2.0 * math.pi / length * phases.astype(jnp.float32)
    return jnp.cos(angles) + jnp.sin(angles)


def symbol_part(length, first_row, count):
    indices = (first_row + lax.iota(jnp.int32, count)) % length
    angles = 2.0 * math.pi / length * indices.astype(jnp.float32)
    return 2.0 - 2.0 * jnp.cos(angles)


def local(log_rate, velocity, initial, profile, plane, depth, row, column, step_of, observed):
    slab, rows, cols = log_rate.shape
    domains, tracers = lax.axis_size("domain"), lax.axis_size("tracer")
    full = slab * domains
    planes = slab + 2 * HALO
    first = lax.axis_index("domain") * slab - HALO
    below, above = halos((log_rate, initial[0]), "domain", HALO)

    keys, values = sort_probes(
        first.reshape(1), planes, full, rows, cols, (depth, row, column, step_of, observed)
    )
    edges = lax.iota(jnp.int32, STEPS * planes + 1) * (rows * cols)
    starts = jnp.sum((keys[None] < edges[:, None, None, None]).astype(jnp.int32), axis=(1, 2, 3))
    place = (plane - first + full) % full

    counts, sums = bins(starts, keys, values, planes, rows, cols)
    coarse = fields(place, velocity, profile[0], log_rate, initial[0], below, above, counts, sums)

    x_size, y_size, z_size = rows // R, cols // R, full // R
    y_own = y_size // (tracers * domains)
    own_first = (lax.axis_index("tracer") * domains + lax.axis_index("domain")) * y_own
    lam = (
        symbol_part(y_size, own_first, y_own)[:, None, None]
        + symbol_part(z_size, 0, z_size)[None, :, None]
        + symbol_part(x_size, 0, x_size)[None, None, :]
    )
    factor = 1.0 + PRIOR_RANGE * lam
    weights = 1.0 / (factor * factor) / (x_size * y_size * z_size)
    tables = [hartley(size, 0, size) for size in (x_size, y_size, z_size)]
    return filtered(coarse, weights, *tables)


def solution(mesh):
    return jax.shard_map(
        local,
        mesh=mesh,
        in_specs=(
            P("domain", None, None),
            P(),
            P("tracer", "domain", None, None),
            P("tracer", None, None),
            P("tracer"),
            P("tracer", None),
            P("tracer", None),
            P("tracer", None),
            P("tracer", None),
            P("tracer", None),
        ),
        out_specs=P("domain", "tracer", None),
        check_vma=False,
    )
```
